256 devices in a mesh: pipe: 8 (over z_lo, y), expert: 16 (over z_hi, x), dp: 2 (over core).
Axes of the slice: x: 4, y: 4, z: 8 (z_hi: 4, z_lo: 2; z = z_hi * 2 + z_lo), core: 2. Of those that a mesh axis runs over, the one named last changes fastest.
Arguments:
- act_in: bfloat16 [8, 1024, 3584], P('pipe', ('expert', 'dp')), may hold values from -6 to 6
- fresh_in: bfloat16 [1024, 3584], P(('expert', 'dp')), may hold values from -6 to 6
- grad_in: bfloat16 [8, 1024, 3584], P('pipe', ('expert', 'dp')), may hold values from -6 to 6
- fresh_grad: bfloat16 [1024, 3584], P(('expert', 'dp')), may hold values from -6 to 6
- saved_input: bfloat16 [2, 8, 1024, 3584], P(None, 'pipe', ('expert', 'dp')), may hold values from -6 to 6
- expert_ids: int32 [8, 4, 1024, 1], P('pipe', None, ('expert', 'dp')), may hold values from 0 to 7, as said below
- slot_ids: int32 [8, 4, 1024, 1], P('pipe', None, ('expert', 'dp')), may hold values from 0 to 5, as said below
- gates: float32 [8, 4, 1024, 1], P('pipe', None, ('expert', 'dp')), may hold values from 0.3 to 2
- up_weight: bfloat16 [8, 3584, 8192], P('pipe', 'dp', 'expert'), may hold values from -0.09375 to 0.09375
- down_weight: bfloat16 [8, 8192, 3584], P('pipe', 'expert', 'dp'), may hold values from -0.1875 to 0.1875
Outputs:
- activations_out: bfloat16 [2, 8, 1024, 3584], P(None, 'pipe', ('expert', 'dp'))
- input_grads: bfloat16 [2, 8, 1024, 3584], P(None, 'pipe', ('expert', 'dp'))
- up_grad: bfloat16 [8, 3584, 8192], P('pipe', 'dp', 'expert')
- down_grad: bfloat16 [8, 8192, 3584], P('pipe', 'expert', 'dp')
The draws below stay inside these ranges and needn't reach their ends.
Inputs may be any that keep to these rules, and one draw needn't show every extreme that they name: `expert_ids`: each token names exactly one expert. Within one aligned block of 32 tokens, for one section and pass, no expert is named more than 6 times, and some expert is named exactly 6 times. `slot_ids`: within one aligned block of 32 tokens, for one section, pass and expert, the tokens naming that expert hold the slots 0, 1, 2 and onward in token order.
All inputs are finite; a program needn't handle non-finite values.
Results may differ from the reference program's by a relative error of at most 0.0065.
Values may be sent and summed in bfloat16 or wider, within the bound.
A program may use at most 128 MiB of HBM per device.

```python
import math
import jax
import jax.numpy as jnp
from jax import lax

D = 3584
HID = 1024
HALVES = 2
TOPK = 1
TOK_DEV = 32
EXPERTS = 8
CAP = 6
TOKENS = 1024
N_PIPE = 8


def routing(key):
    blocks = N_PIPE * 4 * (TOKENS // TOK_DEV)
    subkeys = jax.random.split(jax.random.fold_in(key, 11), 3)
    expert_order = jax.vmap(lambda subkey: jax.random.permutation(subkey, EXPERTS))(jax.random.split(subkeys[0], blocks))
    token_order = jax.vmap(lambda subkey: jax.random.permutation(subkey, TOK_DEV))(jax.random.split(subkeys[1], blocks))
    flip_bits = jax.random.randint(subkeys[2], (blocks, TOK_DEV), 0, 2)
    capacity = CAP
    item_index = jnp.arange(TOPK * TOK_DEV, dtype=jnp.int32)
    item_label = jnp.where(item_index < capacity, 0, 1 + (item_index - capacity) % (EXPERTS - 1))
    item_label = item_label.reshape(TOPK, TOK_DEV).T
    by_position = expert_order[:, item_label]
    inverse = jnp.argsort(token_order, axis=1)
    chosen = jnp.take_along_axis(by_position, inverse[:, :, None], axis=1)
    chosen = jnp.where(flip_bits[:, :, None] == 1, chosen[:, :, ::-1], chosen)
    matches = (chosen[:, :, :, None] == jnp.arange(EXPERTS, dtype=jnp.int32)[None, None, None, :]).astype(jnp.int32)
    per_token = jnp.sum(matches, axis=2)
    before = jnp.cumsum(per_token, axis=1) - per_token
    slot_values = jnp.sum(matches * before[:, :, None, :], axis=3)
    full_shape = (N_PIPE, 4, TOKENS, TOPK)
    return (chosen.reshape(full_shape).astype(jnp.int32), slot_values.reshape(full_shape).astype(jnp.int32))


def draw_expert_ids(key, part):
    return routing(key)[0]


def draw_slot_ids(key, part):
    return routing(key)[1]


def level_of(stream_key, shape, pieces, smallest, high):
    def one(dim, blocks):
        heights = jax.random.uniform(jax.random.fold_in(jax.random.fold_in(stream_key, 6), dim), (blocks,), jnp.float32, smallest / len(pieces), high / len(pieces))
        return jnp.repeat(jnp.exp(heights), shape[dim] // blocks).reshape((-1,) + (1,) * (len(shape) - dim - 1))

    loudness = one(*pieces[0])
    for cut in pieces[1:]:
        loudness = loudness * one(*cut)
    return loudness


def normal_values(stream_key, extent, spread, limit, shards=(), kind=jnp.bfloat16):
    entries = spread * jax.random.normal(stream_key, extent, jnp.float32)
    if shards:
        entries = entries * level_of(stream_key, extent, shards, -0.22, 0.18)
    return jnp.clip(entries, -limit, limit).astype(kind)


def setup_inputs(seed: int = 0) -> dict:
    key_list = jax.random.split(jax.random.key(seed), 11)
    return {
        "act_in": normal_values(key_list[0], (N_PIPE, TOKENS, D), 1.0, 6.0, ((0, 8), (1, 32))),
        "fresh_in": normal_values(key_list[1], (TOKENS, D), 1.0, 6.0, ((0, 32),)),
        "grad_in": normal_values(key_list[2], (N_PIPE, TOKENS, D), 1.0, 6.0, ((0, 8), (1, 32))),
        "fresh_grad": normal_values(key_list[3], (TOKENS, D), 1.0, 6.0, ((0, 32),)),
        "saved_input": normal_values(key_list[4], (2, N_PIPE, TOKENS, D), 1.0, 6.0, ((1, 8), (2, 32))),
        "expert_ids": draw_expert_ids(jax.random.fold_in(key_list[10], 71), 0),
        "slot_ids": draw_slot_ids(jax.random.fold_in(key_list[10], 71), 0),
        "gates": jnp.clip(jnp.exp(math.log(2.0) - 1.89712 * jax.random.uniform(key_list[7], (N_PIPE, 4, TOKENS, TOPK), jnp.float32) ** level_of(key_list[7], (N_PIPE, 4, TOKENS, TOPK), ((0, 8), (2, 32)), -0.2, 0.2)), 0.3, 2.0),
        "up_weight": normal_values(key_list[8], (N_PIPE, D, EXPERTS * HID), D ** -0.5, 0.09375, ((0, 8), (1, 2), (2, 16))),
        "down_weight": normal_values(key_list[9], (N_PIPE, EXPERTS * HID, D), HID ** -0.5, 0.1875, ((0, 8), (1, 16), (2, 2))),
    }


def silu_slope(values):
    logistic = jax.nn.sigmoid(values)
    return logistic * (1.0 + values * (1.0 - logistic))


def slot_tables(chosen, slot_values):
    blocks = TOKENS // TOK_DEV
    block_of = (jnp.arange(TOKENS, dtype=jnp.int32) // TOK_DEV).astype(jnp.int32)
    position = ((chosen * blocks + block_of[:, None]) * CAP + slot_values).reshape(-1).astype(jnp.int32)
    source = jnp.repeat(jnp.arange(TOKENS, dtype=jnp.int32), TOPK)
    source_table = jnp.full((EXPERTS * blocks * CAP,), TOKENS, dtype=jnp.int32).at[position].set(source)
    return position, source_table


def gather_rows(values, source_table):
    padded = jnp.concatenate([values, jnp.zeros((1, D), values.dtype)], axis=0)
    return padded[source_table].reshape(EXPERTS, -1, D)


def mix_back(values, position, gate_rows, expert_out):
    picked = expert_out.reshape(-1, D)[position].reshape(TOKENS, TOPK, D).astype(jnp.float32)
    return (values.astype(jnp.float32) + jnp.sum(gate_rows[:, :, None] * picked, axis=1)).astype(jnp.bfloat16)


def forward_layer(values, up_matrix, down_matrix, chosen, slot_values, gate_rows):
    position, source_table = slot_tables(chosen, slot_values)
    inputs = gather_rows(values, source_table)
    piece = HID // HALVES
    outputs = []
    for expert in range(EXPERTS):
        total = jnp.zeros((inputs.shape[1], D), jnp.float32)
        for half in range(HALVES):
            start = expert * HID + half * piece
            hidden = jax.nn.silu(jnp.dot(inputs[expert], up_matrix[:, start:start + piece], preferred_element_type=jnp.float32)).astype(jnp.bfloat16)
            partial_value = jnp.dot(hidden, down_matrix[start:start + piece], preferred_element_type=jnp.float32).astype(jnp.bfloat16)
            total = total + lax.optimization_barrier(partial_value).astype(jnp.float32)
        outputs.append(total.astype(jnp.bfloat16))
    return mix_back(values, position, gate_rows, jnp.stack(outputs))


def backward_layer(values, upstream, up_matrix, down_matrix, chosen, slot_values, gate_rows):
    position, source_table = slot_tables(chosen, slot_values)
    inputs = gather_rows(values, source_table)
    gate_table = jnp.zeros((source_table.shape[0],), jnp.float32).at[position].set(gate_rows.reshape(-1))
    padded = jnp.concatenate([upstream, jnp.zeros((1, D), upstream.dtype)], axis=0)
    slot_grads = (gate_table[:, None] * padded[source_table].astype(jnp.float32)).astype(jnp.bfloat16).reshape(EXPERTS, -1, D)
    piece = HID // HALVES
    returned = []
    up_parts = []
    down_parts = []
    for expert in range(EXPERTS):
        total = jnp.zeros((inputs.shape[1], D), jnp.float32)
        for half in range(HALVES):
            start = expert * HID + half * piece
            up_piece = up_matrix[:, start:start + piece]
            down_piece = down_matrix[start:start + piece]
            projected = jnp.dot(inputs[expert], up_piece, preferred_element_type=jnp.float32)
            hidden = jax.nn.silu(projected).astype(jnp.bfloat16)
            hidden_grad = jnp.dot(slot_grads[expert], down_piece.T, preferred_element_type=jnp.float32)
            pre_grad = (hidden_grad * silu_slope(projected)).astype(jnp.bfloat16)
            partial_value = jnp.dot(pre_grad, up_piece.T, preferred_element_type=jnp.float32).astype(jnp.bfloat16)
            total = total + lax.optimization_barrier(partial_value).astype(jnp.float32)
            up_parts.append(jnp.dot(inputs[expert].T, pre_grad, preferred_element_type=jnp.float32))
            down_parts.append(jnp.dot(hidden.T, slot_grads[expert], preferred_element_type=jnp.float32))
        returned.append(total.astype(jnp.bfloat16))
    unit_gates = jnp.ones_like(gate_rows)
    input_grad = mix_back(upstream, position, unit_gates, jnp.stack(returned))
    return input_grad, jnp.concatenate(up_parts, axis=1), jnp.concatenate(down_parts, axis=0)


def reference(act_in, fresh_in, grad_in, fresh_grad, saved_input, expert_ids, slot_ids, gates, up_weight, down_weight):
    def run_forward(section_index, values, pass_index):
        return forward_layer(values, up_weight[section_index], down_weight[section_index], expert_ids[section_index, pass_index], slot_ids[section_index, pass_index], gates[section_index, pass_index])

    def run_backward(section_index, values, upstream, pass_index):
        return backward_layer(values, upstream, up_weight[section_index], down_weight[section_index], expert_ids[section_index, pass_index], slot_ids[section_index, pass_index], gates[section_index, pass_index])

    first = [run_forward(section_index, act_in[section_index], 0) for section_index in range(N_PIPE)]
    second = []
    for section_index in range(N_PIPE):
        source_values = fresh_in if section_index == 0 else first[section_index - 1]
        second.append(run_forward(section_index, source_values, 1))
    back_first = [run_backward(section_index, saved_input[0, section_index], grad_in[section_index], 2) for section_index in range(N_PIPE)]
    back_second = []
    for section_index in range(N_PIPE):
        upstream = fresh_grad if section_index == N_PIPE - 1 else back_first[section_index + 1][0]
        back_second.append(run_backward(section_index, saved_input[1, section_index], upstream, 3))
    activations_out = jnp.stack([jnp.stack(first), jnp.stack(second)])
    input_grads = jnp.stack([jnp.stack([item[0] for item in back_first]), jnp.stack([item[0] for item in back_second])])
    up_grad = jnp.stack([(back_first[section_index][1] + back_second[section_index][1]).astype(jnp.bfloat16) for section_index in range(N_PIPE)])
    down_grad = jnp.stack([(back_first[section_index][2] + back_second[section_index][2]).astype(jnp.bfloat16) for section_index in range(N_PIPE)])
    return activations_out, input_grads, up_grad, down_grad
```

```python
import functools

import jax
import jax.numpy as jnp
import numpy as np
from jax import lax
from jax.experimental import pallas as pl
from jax.experimental.pallas import tpu as pltpu
from jax.sharding import PartitionSpec as P

MESH = pl.DeviceIdType.MESH
F32 = jnp.float32
BF16 = jnp.bfloat16
CAP = 6
QUARTERS = 4
SEMS = 140


def regroup_matrix():
    matrix = np.zeros((192, 192), np.float32)
    for z in range(4):
        for pair in range(2):
            for half in range(2):
                for part in range(2):
                    for slot in range(CAP):
                        row = (((pair * 2 + half) * 2 + part) * 4 + z) * CAP + slot
                        column = (((z * 2 + pair) * 2 + half) * 2 + part) * CAP + slot
                        matrix[row, column] = 1.0
    return matrix


def silu_slope(values):
    logistic = jax.nn.sigmoid(values)
    return logistic * (1.0 + values * (1.0 - logistic))


def dot(left, right, dims=((1,), (0,))):
    return lax.dot_general(left, right, (dims, ((), ())), preferred_element_type=F32)


def kernel(
    sections,
    width,
    hidden,
    act_hbm,
    fresh_hbm,
    grad_hbm,
    fresh_grad_hbm,
    saved_hbm,
    up_hbm,
    down_hbm,
    place_ref,
    gate_ref,
    regroup_ref,
    regroup_back_ref,
    acts_out,
    grads_out,
    up_out,
    down_out,
    act,
    fresh,
    grad,
    fresh_grad,
    saved,
    up,
    down,
    select,
    folded,
    z_send,
    z_got,
    z_pass,
    row_send,
    row_got,
    inputs,
    dp_send,
    dp_got,
    hid_kept,
    pre_kept,
    part_own,
    part_send,
    part_got,
    back_send,
    back_got,
    mixed,
    relayed,
    acts_buf,
    grads_buf,
    up_buf,
    down_buf,
    send_sems,
    recv_sems,
    local_sems,
):
    half_width = 2 * width
    section = lax.axis_index("pipe")
    owner = lax.axis_index("expert")
    core = lax.axis_index("dp")
    z = owner // 4
    x = owner % 4
    pair = x // 2
    partner = z * 4 + (x // 2) * 2 + (1 - x % 2)
    across = z * 4 + (3 - x)
    above = ((z + 1) % 4) * 4 + x
    below = ((z + 3) % 4) * 4 + x
    long_to = ((z + 1 + 2 * core) % 4) * 4 + x
    short_to = ((z + 3 - 2 * core) % 4) * 4 + x
    other = 1 - core
    ahead = (section + 1) % sections
    behind = (section + sections - 1) % sections

    loads = {}

    def load(name, source, target, index):
        loads[name] = pltpu.make_async_copy(source, target, local_sems.at[index])
        loads[name].start()

    load("act", act_hbm, act, 0)
    load("saved", saved_hbm, saved, 1)
    load("grad", grad_hbm, grad, 2)
    load("up", up_hbm, up, 3)
    load("down", down_hbm, down, 4)
    load("fresh", fresh_hbm, fresh, 5)
    load("fresh_grad", fresh_grad_hbm, fresh_grad, 6)

    barrier = pltpu.get_barrier_semaphore()
    peers = [{"dp": other}]
    for side in range(2):
        peers.append({"expert": partner, "dp": side})
        peers.append({"expert": across, "dp": side})
    peers += [{"expert": above}, {"expert": below}, {"pipe": ahead}, {"pipe": behind}]
    if sections == 2:
        peers = peers[:-1]
    for peer in peers:
        pl.semaphore_signal(barrier, inc=1, device_id=peer, device_id_type=MESH)

    def selection(which):
        place = place_ref[which : which + 1, :]
        expert = place >> 3
        slot = place & 7
        lane = lax.broadcasted_iota(jnp.int32, (1, 128), 1)
        z_steps = ((expert >> 1) + 4 - z) & 3
        flipped = (expert & 1) ^ pair
        row = z_steps * 48 + flipped * 24 + (lane >> 5) * CAP + slot
        rows = lax.broadcasted_iota(jnp.int32, (192, 128), 0)
        select[which] = jnp.where(rows == row, 1.0, 0.0).astype(BF16)

    def gate_column(which):
        row = gate_ref[which : which + 1, :]
        diagonal = lax.broadcasted_iota(jnp.int32, (128, 128), 0) == lax.broadcasted_iota(
            jnp.int32, (128, 128), 1
        )
        return jnp.sum(jnp.where(diagonal, row, 0.0), axis=1, keepdims=True)

    copies = []

    def remote(source, target, device):
        index = len(copies)
        copy = pltpu.make_async_remote_copy(
            src_ref=source,
            dst_ref=target,
            send_sem=send_sems.at[index],
            recv_sem=recv_sems.at[index],
            device_id=device,
            device_id_type=MESH,
        )
        copy.start()
        copies.append(copy)
        return copy

    def fold(values, slot):
        for quarter in range(QUARTERS):
            folded[slot, quarter * 32 : quarter * 32 + 32, :] = values[
                :, quarter * width : (quarter + 1) * width
            ]

    def z_start(e):
        return [
            remote(z_send.at[e, pl.ds(0, 48)], z_got.at[e, pl.ds(144, 48)], {"expert": above}),
            remote(z_send.at[e, pl.ds(96, 48)], z_got.at[e, pl.ds(48, 48)], {"expert": below}),
            remote(z_send.at[e, pl.ds(48, 32)], z_pass.at[e, pl.ds(0, 32)], {"expert": long_to}),
            remote(z_send.at[e, pl.ds(80, 16)], z_pass.at[e, pl.ds(32, 16)], {"expert": short_to}),
        ]

    def z_forward(e, started):
        started[2].wait_recv()
        started.append(
            remote(z_pass.at[e, pl.ds(0, 32)], z_got.at[e, pl.ds(96, 32)], {"expert": long_to})
        )
        started[3].wait_recv()
        started.append(
            remote(z_pass.at[e, pl.ds(32, 16)], z_got.at[e, pl.ds(128, 16)], {"expert": short_to})
        )

    def z_finish(started):
        for item in (0, 1, 4, 5):
            started[item].wait_recv()

    def dispatch(u, which, slot):
        rows = dot(select[which], folded[slot]).astype(BF16)
        z_got[u, 0:48, :] = rows[0:48]
        z_send[u] = rows[48:192]
        return z_start(u)

    def spread(u, started):
        z_finish(started)
        rows = dot(regroup_ref[...], z_got[u]).astype(BF16)
        for item in range(4):
            row_send[u, item] = rows[48 * item : 48 * item + 48]
        row_got[u, core] = row_send[u, core]
        return [
            remote(row_send.at[u, 2 + core], row_got.at[u, 2 + core], {"expert": across}),
            remote(
                row_send.at[u, 2 + other], row_got.at[u, 2 + core], {"expert": across, "dp": other}
            ),
            remote(row_send.at[u, core], row_got.at[u, 4 + core], {"expert": partner}),
            remote(
                row_send.at[u, other], row_got.at[u, 4 + core], {"expert": partner, "dp": other}
            ),
            remote(row_send.at[u, other], row_got.at[u, core], {"dp": other}),
        ]

    def spread_forward(u, sent):
        sent[0].wait_recv()
        sent.append(
            remote(row_got.at[u, 2 + core], row_got.at[u, 6 + core], {"expert": partner})
        )
        sent[1].wait_recv()
        sent.append(
            remote(row_got.at[u, 2 + other], row_got.at[u, 6 + other], {"expert": partner})
        )

    def gather(u, sent, place):
        for item in range(2, 7):
            sent[item].wait_recv()
        for both in range(4):
            first = row_got[u, 2 * both].astype(F32)
            second = row_got[u, 2 * both + 1].astype(F32)
            start = 192 * place + 48 * both
            for part in range(2):
                rows = jnp.concatenate(
                    [first[24 * part : 24 * part + 24], second[24 * part : 24 * part + 24]], axis=0
                )
                inputs[start : start + 48, part * width : (part + 1) * width] = rows.astype(BF16)

    def unit_rows(place):
        return inputs[192 * place : 192 * place + 192, :]

    def share_sum(item, partial_sum):
        dp_send[item] = partial_sum
        return remote(dp_send.at[item], dp_got.at[item], {"dp": other})

    def full_sum(item, copy):
        copy.wait_recv()
        return dp_send[item] + dp_got[item]

    def halves_start(c, product):
        part_send[c] = product(96).astype(BF16)
        copy = remote(part_send.at[c], part_got.at[c], {"expert": partner})
        part_own[c] = product(0).astype(BF16)
        return copy

    def halves_sum(c, copy):
        copy.wait_recv()
        for item in (2, 3, 0, 1):
            total = part_own[c, 48 * (item // 2) : 48 * (item // 2) + 48].astype(F32)
            total = total + part_got[c, 48 * (item // 2) : 48 * (item // 2) + 48].astype(F32)
            total = total[24 * (item % 2) : 24 * (item % 2) + 24]
            back_send[c, item] = jnp.concatenate(
                [total[:, :width], total[:, width:]], axis=0
            ).astype(BF16)
        back_got[c, core] = back_send[c, core]
        return [
            remote(back_send.at[c, 2 + core], back_got.at[c, 2 + core], {"expert": across}),
            remote(
                back_send.at[c, 2 + other],
                back_got.at[c, 2 + core],
                {"expert": across, "dp": other},
            ),
            remote(back_send.at[c, other], back_got.at[c, core], {"dp": other}),
        ]

    def returning(c, sent):
        for copy in sent:
            copy.wait_recv()
        gathered = jnp.concatenate([back_got[c, item] for item in range(4)], axis=0)
        rows = dot(regroup_back_ref[...], gathered).astype(BF16)
        z_got[6 + c, 0:48, :] = rows[0:48]
        z_send[6 + c] = rows[48:192]
        return z_start(6 + c)

    def mix(c, which, slot, gated, started):
        z_finish(started)
        picked = dot(select[which], z_got[6 + c], ((0,), (0,)))
        if gated:
            picked = gate_column(which) * picked
        mixed[c] = (folded[slot].astype(F32) + picked).astype(BF16)

    def give_out(c, buffer, target, which, index):
        for quarter in range(QUARTERS):
            buffer[which, :, quarter * width : (quarter + 1) * width] = mixed[
                c, quarter * 32 : quarter * 32 + 32, :
            ]
        copy = pltpu.make_async_copy(buffer.at[which], target.at[which], local_sems.at[index])
        copy.start()
        return copy

    def gate_folded(which, source, target):
        folded[target] = (gate_column(which) * folded[source].astype(F32)).astype(BF16)

    def forward_up(item, place):
        return share_sum(item, dot(unit_rows(place), up[...]))

    def forward_down(c, item, copy):
        active = jax.nn.silu(full_sum(item, copy)).astype(BF16)
        return halves_start(c, lambda start: dot(active[start : start + 96], down[...]))

    def grad_down(item, place):
        return share_sum(item, dot(unit_rows(place), down[...], ((1,), (1,))))

    def backward_up(c, step, items, sums):
        projected = full_sum(items[0], sums[0])
        rows = slice(192 * step, 192 * step + 192)
        hid_kept[rows] = jax.nn.silu(projected).astype(BF16)
        slope = silu_slope(projected)
        pre_grad = (full_sum(items[1], sums[1]) * slope).astype(BF16)
        pre_kept[rows] = pre_grad
        return halves_start(
            c, lambda start: dot(pre_grad[start : start + 96], up[...], ((1,), (1,)))
        )

    selection(0)
    loads["act"].wait()
    fold(act, 0)
    pl.semaphore_wait(barrier, len(peers))
    z0 = dispatch(0, 0, 0)
    selection(2)
    loads["saved"].wait()
    fold(saved.at[0], 1)
    z1 = dispatch(1, 2, 1)
    loads["grad"].wait()
    fold(grad, 6)
    gate_folded(2, 6, 2)
    z2 = dispatch(2, 2, 2)
    selection(1)
    selection(3)
    fold(saved.at[1], 3)
    z_forward(0, z0)
    r0 = spread(0, z0)
    z_forward(1, z1)
    spread_forward(0, r0)
    r1 = spread(1, z1)
    z_forward(2, z2)
    loads["up"].wait()
    loads["down"].wait()
    gather(0, r0, 4)
    d0 = forward_up(0, 4)
    spread_forward(1, r1)
    r2 = spread(2, z2)
    p0 = forward_down(0, 0, d0)
    z3 = dispatch(3, 3, 3)
    spread_forward(2, r2)
    gather(1, r1, 0)
    d1 = forward_up(1, 0)
    b0 = halves_sum(0, p0)
    gather(2, r2, 2)
    d2 = grad_down(2, 2)
    y0 = returning(0, b0)
    p1 = backward_up(1, 0, (1, 2), (d1, d2))
    z_forward(6, y0)
    z_forward(3, z3)
    loads["fresh"].wait()
    loads["fresh_grad"].wait()
    mix(0, 0, 0, True, y0)
    up_copy = remote(mixed.at[0], relayed.at[0], {"pipe": ahead})
    b1 = halves_sum(1, p1)
    out0 = give_out(0, acts_buf, acts_out, 0, 7)
    y1 = returning(1, b1)
    r3 = spread(3, z3)
    fold(fresh, 4)
    up_copy.wait_recv()
    folded[4] = jnp.where(section == 0, folded[4], relayed[0])
    z4 = dispatch(4, 1, 4)
    z_forward(7, y1)
    mix(1, 2, 6, False, y1)
    down_copy = remote(mixed.at[1], relayed.at[1], {"pipe": behind})
    out1 = give_out(1, grads_buf, grads_out, 0, 8)
    fold(fresh_grad, 7)
    z_forward(4, z4)
    spread_forward(3, r3)
    r4 = spread(4, z4)
    down_copy.wait_recv()
    folded[7] = jnp.where(section == sections - 1, folded[7], relayed[1])
    gate_folded(3, 7, 5)
    z5 = dispatch(5, 3, 5)
    spread_forward(4, r4)
    gather(3, r3, 1)
    d4 = forward_up(4, 1)
    z_forward(5, z5)
    gather(4, r4, 5)
    d3 = forward_up(3, 5)
    r5 = spread(5, z5)
    p2 = forward_down(2, 3, d3)
    spread_forward(5, r5)
    b2 = halves_sum(2, p2)
    gather(5, r5, 3)
    d5 = grad_down(5, 3)
    y2 = returning(2, b2)
    p3 = backward_up(3, 1, (4, 5), (d4, d5))
    z_forward(8, y2)

    def up_tile(step, carry):
        start = pl.multiple_of(step * 256, 256)
        up_buf[pl.ds(start, 256), :] = dot(
            inputs[0:384, pl.ds(start, 256)], pre_kept[...], ((0,), (0,))
        ).astype(BF16)
        return carry

    lax.fori_loop(0, half_width // 256, up_tile, 0)
    out_up = pltpu.make_async_copy(up_buf, up_out, local_sems.at[11])
    out_up.start()
    b3 = halves_sum(3, p3)
    mix(2, 1, 4, True, y2)
    out2 = give_out(2, acts_buf, acts_out, 1, 9)
    y3 = returning(3, b3)
    for part in range(2):
        columns = slice(part * width, (part + 1) * width)
        down_buf[:, columns] = dot(hid_kept[...], inputs[384:768, columns], ((0,), (0,))).astype(
            BF16
        )
    out_down = pltpu.make_async_copy(down_buf, down_out, local_sems.at[12])
    out_down.start()
    z_forward(9, y3)
    mix(3, 3, 7, False, y3)
    out3 = give_out(3, grads_buf, grads_out, 1, 10)
    for copy in copies:
        copy.wait_send()
    for copy in (out0, out1, out2, out3, out_up, out_down):
        copy.wait()
    assert len(copies) <= SEMS


def per_device(
    act_in,
    fresh_in,
    grad_in,
    fresh_grad,
    saved_input,
    expert_ids,
    slot_ids,
    gates,
    up_weight,
    down_weight,
):
    sections = lax.axis_size("pipe")
    tokens, features = fresh_in.shape
    width = features // QUARTERS
    hidden = up_weight.shape[2]
    place = jnp.tile(expert_ids[0, :, :, 0] * 8 + slot_ids[0, :, :, 0], (1, QUARTERS))
    gate_rows = jnp.tile(gates[0, :, :, 0], (1, QUARTERS))
    regroup = regroup_matrix()
    anywhere = pl.BlockSpec(memory_space=pl.ANY)
    in_vmem = pl.BlockSpec(memory_space=pltpu.VMEM)
    full = (tokens, features)
    vm = pltpu.VMEM
    acts, grads, up_grad, down_grad = pl.pallas_call(
        functools.partial(kernel, sections, width, hidden),
        out_shape=(
            jax.ShapeDtypeStruct((2,) + full, BF16),
            jax.ShapeDtypeStruct((2,) + full, BF16),
            jax.ShapeDtypeStruct((2 * width, hidden), BF16),
            jax.ShapeDtypeStruct((hidden, 2 * width), BF16),
        ),
        in_specs=[anywhere] * 7 + [in_vmem] * 4,
        out_specs=[anywhere] * 4,
        scratch_shapes=[
            vm(full, BF16),
            vm(full, BF16),
            vm(full, BF16),
            vm(full, BF16),
            vm((2,) + full, BF16),
            vm((2 * width, hidden), BF16),
            vm((hidden, 2 * width), BF16),
            vm((4, 192, 128), BF16),
            vm((8, 128, width), BF16),
            vm((10, 144, width), BF16),
            vm((10, 192, width), BF16),
            vm((10, 48, width), BF16),
            vm((6, 4, 48, width), BF16),
            vm((6, 8, 48, width), BF16),
            vm((1152, 2 * width), BF16),
            vm((6, 192, hidden), F32),
            vm((6, 192, hidden), F32),
            vm((384, hidden), BF16),
            vm((384, hidden), BF16),
            vm((4, 96, 2 * width), BF16),
            vm((4, 96, 2 * width), BF16),
            vm((4, 96, 2 * width), BF16),
            vm((4, 4, 48, width), BF16),
            vm((4, 4, 48, width), BF16),
            vm((4, 128, width), BF16),
            vm((2, 128, width), BF16),
            vm((2,) + full, BF16),
            vm((2,) + full, BF16),
            vm((2 * width, hidden), BF16),
            vm((hidden, 2 * width), BF16),
            pltpu.SemaphoreType.DMA((SEMS,)),
            pltpu.SemaphoreType.DMA((SEMS,)),
            pltpu.SemaphoreType.DMA((13,)),
        ],
        compiler_params=pltpu.CompilerParams(
            collective_id=0, has_side_effects=True, vmem_limit_bytes=60 * 2**20
        ),
    )(
        act_in[0],
        fresh_in,
        grad_in[0],
        fresh_grad,
        saved_input[:, 0],
        up_weight[0],
        down_weight[0],
        place,
        gate_rows,
        jnp.asarray(regroup, BF16),
        jnp.asarray(regroup.T, BF16),
    )
    return acts[:, None], grads[:, None], up_grad[None], down_grad[None]


def solution(mesh):
    in_specs = (
        P("pipe", ("expert", "dp"), None),
        P(("expert", "dp"), None),
        P("pipe", ("expert", "dp"), None),
        P(("expert", "dp"), None),
        P(None, "pipe", ("expert", "dp"), None),
        P("pipe", None, ("expert", "dp"), None),
        P("pipe", None, ("expert", "dp"), None),
        P("pipe", None, ("expert", "dp"), None),
        P("pipe", "dp", "expert"),
        P("pipe", "expert", "dp"),
    )
    out_specs = (
        P(None, "pipe", ("expert", "dp"), None),
        P(None, "pipe", ("expert", "dp"), None),
        P("pipe", "dp", "expert"),
        P("pipe", "expert", "dp"),
    )
    return jax.shard_map(
        per_device, mesh=mesh, in_specs=in_specs, out_specs=out_specs, check_vma=False
    )
```

```python
import functools

import jax
import jax.numpy as jnp
import numpy as np
from jax import lax
from jax.experimental import pallas as pl
from jax.experimental.pallas import tpu as pltpu
from jax.sharding import PartitionSpec as P

MESH = pl.DeviceIdType.MESH
F32 = jnp.float32
BF16 = jnp.bfloat16
CAP = 6
QUARTERS = 4
SEMS = 310
CHUNKS = 2


def regroup_matrix():
    matrix = np.zeros((192, 192), np.float32)
    for z in range(4):
        for pair in range(2):
            for half in range(2):
                for part in range(2):
                    for slot in range(CAP):
                        row = (((pair * 2 + half) * 2 + part) * 4 + z) * CAP + slot
                        column = (((z * 2 + pair) * 2 + half) * 2 + part) * CAP + slot
                        matrix[row, column] = 1.0
    return matrix


def silu_slope(values):
    logistic = jax.nn.sigmoid(values)
    return logistic * (1.0 + values * (1.0 - logistic))


def dot(left, right, dims=((1,), (0,))):
    return lax.dot_general(left, right, (dims, ((), ())), preferred_element_type=F32)


def kernel(
    sections,
    width,
    hidden,
    act_hbm,
    fresh_hbm,
    grad_hbm,
    fresh_grad_hbm,
    saved_hbm,
    up_hbm,
    down_hbm,
    place_ref,
    gate_ref,
    regroup_ref,
    regroup_back_ref,
    acts_out,
    grads_out,
    up_out,
    down_out,
    act,
    fresh,
    grad,
    fresh_grad,
    saved,
    up,
    down,
    select,
    folded,
    z_send,
    z_got,
    row_send,
    row_got,
    inputs,
    dp_send,
    dp_got,
    hid_kept,
    pre_kept,
    back_send,
    back_got,
    mixed,
    relayed,
    acts_buf,
    grads_buf,
    up_buf,
    down_buf,
    send_sems,
    recv_sems,
    local_sems,
):
    half_width = 2 * width
    section = lax.axis_index("pipe")
    owner = lax.axis_index("expert")
    core = lax.axis_index("dp")
    z = owner // 4
    x = owner % 4
    pair = x // 2
    partner = z * 4 + pair * 2 + (1 - x % 2)
    across = z * 4 + (3 - x)
    diagonal = z * 4 + (x + 2) % 4
    above = ((z + 1) % 4) * 4 + x
    below = ((z + 3) % 4) * 4 + x
    opposite = ((z + 2) % 4) * 4 + x
    other = 1 - core
    ahead = (section + 1) % sections
    behind = (section + sections - 1) % sections

    loads = {}

    def load(name, source, target, index):
        loads[name] = pltpu.make_async_copy(source, target, local_sems.at[index])
        loads[name].start()

    load("act", act_hbm, act, 0)
    load("saved", saved_hbm, saved, 1)
    load("grad", grad_hbm, grad, 2)
    load("up", up_hbm, up, 3)
    load("down", down_hbm, down, 4)
    load("fresh", fresh_hbm, fresh, 5)
    load("fresh_grad", fresh_grad_hbm, fresh_grad, 6)

    barrier = pltpu.get_barrier_semaphore()
    peers = [{"dp": other}]
    for owner_there in (partner, across, diagonal):
        peers.append({"expert": owner_there})
        peers.append({"expert": owner_there, "dp": other})
    for owner_there in (above, below, opposite):
        peers.append({"expert": owner_there})
    peers += [{"pipe": ahead}, {"pipe": behind}]
    if sections == 2:
        peers = peers[:-1]
    for peer in peers:
        pl.semaphore_signal(barrier, inc=1, device_id=peer, device_id_type=MESH)

    def selection(which):
        place = place_ref[which : which + 1, :]
        expert = place >> 3
        slot = place & 7
        lane = lax.broadcasted_iota(jnp.int32, (1, 128), 1)
        z_steps = ((expert >> 1) + 4 - z) & 3
        flipped = (expert & 1) ^ pair
        row = z_steps * 48 + flipped * 24 + (lane >> 5) * CAP + slot
        rows = lax.broadcasted_iota(jnp.int32, (192, 128), 0)
        select[which] = jnp.where(rows == row, 1.0, 0.0).astype(BF16)

    def gate_column(which):
        row = gate_ref[which : which + 1, :]
        on_diagonal = lax.broadcasted_iota(jnp.int32, (128, 128), 0) == lax.broadcasted_iota(
            jnp.int32, (128, 128), 1
        )
        return jnp.sum(jnp.where(on_diagonal, row, 0.0), axis=1, keepdims=True)

    copies = []

    def remote(source, target, device):
        index = len(copies)
        copy = pltpu.make_async_remote_copy(
            src_ref=source,
            dst_ref=target,
            send_sem=send_sems.at[index],
            recv_sem=recv_sems.at[index],
            device_id=device,
            device_id_type=MESH,
        )
        copy.start()
        copies.append(copy)
        return copy

    def fold(values, slot):
        for quarter in range(QUARTERS):
            folded[slot, quarter * 32 : quarter * 32 + 32, :] = values[
                :, quarter * width : (quarter + 1) * width
            ]

    def z_start(e, lanes):
        return [
            remote(
                z_send.at[e, pl.ds(start, 48), lanes],
                z_got.at[e, pl.ds(192 - 48 - start, 48), lanes],
                {"expert": device},
            )
            for start, device in ((48, opposite), (0, above), (96, below))
        ]

    def finish(started):
        for copy in started:
            copy.wait_recv()

    def span(lanes, part):
        return pl.ds(part * width + lanes.start, lanes.size)

    def dispatch(u, which, slot, lanes):
        rows = dot(select[which], folded[slot, :, lanes]).astype(BF16)
        z_got[u, 0:48, lanes] = rows[0:48]
        z_send[u, :, lanes] = rows[48:192]
        return z_start(u, lanes)

    def spread(u, started, lanes):
        finish(started)
        rows = dot(regroup_ref[...], z_got[u, :, lanes]).astype(BF16)
        for item in range(4):
            row_send[u, item, :, lanes] = rows[48 * item : 48 * item + 48]
        row_got[u, core, :, lanes] = row_send[u, core, :, lanes]

        def to(source, target, device):
            return remote(row_send.at[u, source, :, lanes], row_got.at[u, target, :, lanes], device)

        return [
            to(2 + core, 6 + core, {"expert": diagonal}),
            to(2 + other, 6 + core, {"expert": diagonal, "dp": other}),
            to(core, 4 + core, {"expert": partner}),
            to(other, 4 + core, {"expert": partner, "dp": other}),
            to(2 + core, 2 + core, {"expert": across}),
            to(2 + other, 2 + core, {"expert": across, "dp": other}),
            to(other, core, {"dp": other}),
        ]

    def gather(u, sent, place, lanes):
        finish(sent)
        for both in range(4):
            first = row_got[u, 2 * both, :, lanes].astype(F32)
            second = row_got[u, 2 * both + 1, :, lanes].astype(F32)
            start = 192 * place + 48 * both
            for part in range(2):
                rows = jnp.concatenate(
                    [first[24 * part : 24 * part + 24], second[24 * part : 24 * part + 24]], axis=0
                )
                inputs[start : start + 48, span(lanes, part)] = rows.astype(BF16)

    def times_up(place, lanes):
        rows = pl.ds(192 * place, 192)
        return sum(
            dot(inputs[rows, span(lanes, part)], up[span(lanes, part), :]) for part in range(2)
        )

    def times_down(place, lanes):
        rows = pl.ds(192 * place, 192)
        return sum(
            dot(inputs[rows, span(lanes, part)], down[:, span(lanes, part)], ((1,), (1,)))
            for part in range(2)
        )

    def share_sum(item, partial_sum):
        dp_send[item] = partial_sum
        return remote(dp_send.at[item], dp_got.at[item], {"dp": other})

    def full_sum(item, copy):
        copy.wait_recv()
        return dp_send[item] + dp_got[item]

    def give_back(c, product, lanes):
        parts = [product(span(lanes, part)) for part in range(2)]
        for item in (6, 7, 4, 5, 2, 3, 0, 1):
            rows = slice(24 * item, 24 * item + 24)
            back_send[c, item, :, lanes] = jnp.concatenate(
                [parts[0][rows], parts[1][rows]], axis=0
            ).astype(BF16)
        back_got[c, core, :, lanes] = back_send[c, core, :, lanes]

        def to(source, target, device):
            return remote(
                back_send.at[c, source, :, lanes], back_got.at[c, target, :, lanes], device
            )

        return [
            to(6 + core, 6 + core, {"expert": diagonal}),
            to(6 + other, 6 + core, {"expert": diagonal, "dp": other}),
            to(4 + core, 4 + core, {"expert": partner}),
            to(4 + other, 4 + core, {"expert": partner, "dp": other}),
            to(2 + core, 2 + core, {"expert": across}),
            to(2 + other, 2 + core, {"expert": across, "dp": other}),
            to(other, core, {"dp": other}),
        ]

    def returning(c, sent, lanes):
        finish(sent)
        totals = [
            (
                back_got[c, item, :, lanes].astype(F32) + back_got[c, item + 4, :, lanes].astype(F32)
            ).astype(BF16)
            for item in range(4)
        ]
        rows = dot(regroup_back_ref[...], jnp.concatenate(totals, axis=0)).astype(BF16)
        z_got[6 + c, 0:48, lanes] = rows[0:48]
        z_send[6 + c, :, lanes] = rows[48:192]
        return z_start(6 + c, lanes)

    def mix(c, which, slot, gated, started, lanes):
        finish(started)
        picked = dot(select[which], z_got[6 + c, :, lanes], ((0,), (0,)))
        if gated:
            picked = gate_column(which) * picked
        mixed[c, :, lanes] = (folded[slot, :, lanes].astype(F32) + picked).astype(BF16)

    def relay(item, device, lanes):
        return remote(mixed.at[item, :, lanes], relayed.at[item, :, lanes], {"pipe": device})

    def give_out(c, buffer, target, which, index):
        for quarter in range(QUARTERS):
            buffer[which, :, quarter * width : (quarter + 1) * width] = mixed[
                c, quarter * 32 : quarter * 32 + 32, :
            ]
        copy = pltpu.make_async_copy(buffer.at[which], target.at[which], local_sems.at[index])
        copy.start()
        return copy

    def gate_folded(which, source, target, lanes):
        folded[target, :, lanes] = (
            gate_column(which) * folded[source, :, lanes].astype(F32)
        ).astype(BF16)

    def receive(item, slot, at_end, copy, lanes):
        copy.wait_recv()
        folded[slot, :, lanes] = jnp.where(
            at_end, folded[slot, :, lanes], relayed[item, :, lanes]
        )

    groups = width // 128
    count = min(CHUNKS, groups)
    edges = [-(-groups * item // count) * 128 for item in range(count + 1)]
    chunks = [pl.ds(edges[item], edges[item + 1] - edges[item]) for item in range(count)]
    whole = pl.ds(0, width)
    every = range(count)

    selection(0)
    loads["act"].wait()
    fold(act, 0)
    pl.semaphore_wait(barrier, len(peers))
    z0 = [dispatch(0, 0, 0, lanes) for lanes in chunks]
    selection(2)
    loads["saved"].wait()
    fold(saved.at[0], 1)
    loads["grad"].wait()
    fold(grad, 6)
    gate_folded(2, 6, 2, whole)
    r0, r1, r2, r3, r4, r5 = [], [], [], [], [], []
    z1, z2, z3, z4, z5 = [], [], [], [], []
    for n in every:
        r0.append(spread(0, z0[n], chunks[n]))
        z1.append(dispatch(1, 2, 1, chunks[n]))
    selection(3)
    selection(1)
    fold(saved.at[1], 3)
    loads["up"].wait()
    loads["down"].wait()
    total = None
    for n in every:
        gather(0, r0[n], 4, chunks[n])
        product = times_up(4, chunks[n])
        total = product if total is None else total + product
        if n == count - 1:
            d0 = share_sum(0, total)
        r1.append(spread(1, z1[n], chunks[n]))
        z2.append(dispatch(2, 2, 2, chunks[n]))
    active = jax.nn.silu(full_sum(0, d0)).astype(BF16)
    p0 = [
        give_back(0, lambda columns: dot(active, down[:, columns]), lanes) for lanes in chunks
    ]
    for n in every:
        r2.append(spread(2, z2[n], chunks[n]))
        z3.append(dispatch(3, 3, 3, chunks[n]))
    total = None
    for lanes, copies_in in zip(chunks, r1):
        gather(1, copies_in, 0, lanes)
        product = times_up(0, lanes)
        total = product if total is None else total + product
    d1 = share_sum(1, total)
    y0 = [returning(0, p0[n], chunks[n]) for n in every]
    total = None
    for lanes, copies_in in zip(chunks, r2):
        gather(2, copies_in, 2, lanes)
        product = times_down(2, lanes)
        total = product if total is None else total + product
    d2 = share_sum(2, total)
    loads["fresh"].wait()
    loads["fresh_grad"].wait()
    fold(fresh, 4)
    fold(fresh_grad, 7)

    def backward_up(c, step, items, sums):
        projected = full_sum(items[0], sums[0])
        rows = slice(192 * step, 192 * step + 192)
        hid_kept[rows] = jax.nn.silu(projected).astype(BF16)
        slope = silu_slope(projected)
        pre_grad = (full_sum(items[1], sums[1]) * slope).astype(BF16)
        pre_kept[rows] = pre_grad
        return [
            give_back(c, lambda columns: dot(pre_grad, up[columns, :], ((1,), (1,))), lanes)
            for lanes in chunks
        ]

    p1 = backward_up(1, 0, (1, 2), (d1, d2))
    up_copies = []
    for n in every:
        mix(0, 0, 0, True, y0[n], chunks[n])
        up_copies.append(relay(0, ahead, chunks[n]))
    out0 = give_out(0, acts_buf, acts_out, 0, 7)
    y1 = [returning(1, p1[n], chunks[n]) for n in every]
    for n in every:
        receive(0, 4, section == 0, up_copies[n], chunks[n])
        z4.append(dispatch(4, 1, 4, chunks[n]))
    for n in every:
        r3.append(spread(3, z3[n], chunks[n]))
    down_copies = []
    for n in every:
        mix(1, 2, 6, False, y1[n], chunks[n])
        down_copies.append(relay(1, behind, chunks[n]))
    out1 = give_out(1, grads_buf, grads_out, 0, 8)
    for n in every:
        receive(1, 7, section == sections - 1, down_copies[n], chunks[n])
        gate_folded(3, 7, 5, chunks[n])
        z5.append(dispatch(5, 3, 5, chunks[n]))
    for n in every:
        r4.append(spread(4, z4[n], chunks[n]))
    total = None
    for lanes, copies_in in zip(chunks, r3):
        gather(3, copies_in, 1, lanes)
        product = times_up(1, lanes)
        total = product if total is None else total + product
    d4 = share_sum(4, total)
    total = None
    for n in every:
        gather(4, r4[n], 5, chunks[n])
        product = times_up(5, chunks[n])
        total = product if total is None else total + product
        if n == count - 1:
            d3 = share_sum(3, total)
        r5.append(spread(5, z5[n], chunks[n]))
    active_later = jax.nn.silu(full_sum(3, d3)).astype(BF16)
    p2 = [
        give_back(2, lambda columns: dot(active_later, down[:, columns]), lanes)
        for lanes in chunks
    ]
    total = None
    for lanes, copies_in in zip(chunks, r5):
        gather(5, copies_in, 3, lanes)
        product = times_down(3, lanes)
        total = product if total is None else total + product
    d5 = share_sum(5, total)
    y2 = [returning(2, p2[n], chunks[n]) for n in every]
    p3 = backward_up(3, 1, (4, 5), (d4, d5))

    def up_tile(step, carry):
        start = pl.multiple_of(step * 256, 256)
        up_buf[pl.ds(start, 256), :] = dot(
            inputs[0:384, pl.ds(start, 256)], pre_kept[...], ((0,), (0,))
        ).astype(BF16)
        return carry

    lax.fori_loop(0, half_width // 256, up_tile, 0)
    out_up = pltpu.make_async_copy(up_buf, up_out, local_sems.at[11])
    out_up.start()
    for n in every:
        mix(2, 1, 4, True, y2[n], chunks[n])
    out2 = give_out(2, acts_buf, acts_out, 1, 9)
    y3 = [returning(3, p3[n], chunks[n]) for n in every]
    for part in range(2):
        columns = slice(part * width, (part + 1) * width)
        down_buf[:, columns] = dot(hid_kept[...], inputs[384:768, columns], ((0,), (0,))).astype(
            BF16
        )
    out_down = pltpu.make_async_copy(down_buf, down_out, local_sems.at[12])
    out_down.start()
    for n in every:
        mix(3, 3, 7, False, y3[n], chunks[n])
    out3 = give_out(3, grads_buf, grads_out, 1, 10)
    for copy in copies:
        copy.wait_send()
    for copy in (out0, out1, out2, out3, out_up, out_down):
        copy.wait()
    assert len(copies) <= SEMS


def per_device(
    act_in,
    fresh_in,
    grad_in,
    fresh_grad,
    saved_input,
    expert_ids,
    slot_ids,
    gates,
    up_weight,
    down_weight,
):
    sections = lax.axis_size("pipe")
    tokens, features = fresh_in.shape
    width = features // QUARTERS
    hidden = up_weight.shape[2]
    place = jnp.tile(expert_ids[0, :, :, 0] * 8 + slot_ids[0, :, :, 0], (1, QUARTERS))
    gate_rows = jnp.tile(gates[0, :, :, 0], (1, QUARTERS))
    regroup = regroup_matrix()
    anywhere = pl.BlockSpec(memory_space=pl.ANY)
    in_vmem = pl.BlockSpec(memory_space=pltpu.VMEM)
    full = (tokens, features)
    vm = pltpu.VMEM
    acts, grads, up_grad, down_grad = pl.pallas_call(
        functools.partial(kernel, sections, width, hidden),
        out_shape=(
            jax.ShapeDtypeStruct((2,) + full, BF16),
            jax.ShapeDtypeStruct((2,) + full, BF16),
            jax.ShapeDtypeStruct((2 * width, hidden), BF16),
            jax.ShapeDtypeStruct((hidden, 2 * width), BF16),
        ),
        in_specs=[anywhere] * 7 + [in_vmem] * 4,
        out_specs=[anywhere] * 4,
        scratch_shapes=[
            vm(full, BF16),
            vm(full, BF16),
            vm(full, BF16),
            vm(full, BF16),
            vm((2,) + full, BF16),
            vm((2 * width, hidden), BF16),
            vm((hidden, 2 * width), BF16),
            vm((4, 192, 128), BF16),
            vm((8, 128, width), BF16),
            vm((10, 144, width), BF16),
            vm((10, 192, width), BF16),
            vm((6, 4, 48, width), BF16),
            vm((6, 8, 48, width), BF16),
            vm((1152, 2 * width), BF16),
            vm((6, 192, hidden), F32),
            vm((6, 192, hidden), F32),
            vm((384, hidden), BF16),
            vm((384, hidden), BF16),
            vm((4, 8, 48, width), BF16),
            vm((4, 8, 48, width), BF16),
            vm((4, 128, width), BF16),
            vm((2, 128, width), BF16),
            vm((2,) + full, BF16),
            vm((2,) + full, BF16),
            vm((2 * width, hidden), BF16),
            vm((hidden, 2 * width), BF16),
            pltpu.SemaphoreType.DMA((SEMS,)),
            pltpu.SemaphoreType.DMA((SEMS,)),
            pltpu.SemaphoreType.DMA((13,)),
        ],
        compiler_params=pltpu.CompilerParams(
            collective_id=0, has_side_effects=True, vmem_limit_bytes=60 * 2**20
        ),
    )(
        act_in[0],
        fresh_in,
        grad_in[0],
        fresh_grad,
        saved_input[:, 0],
        up_weight[0],
        down_weight[0],
        place,
        gate_rows,
        jnp.asarray(regroup, BF16),
        jnp.asarray(regroup.T, BF16),
    )
    return acts[:, None], grads[:, None], up_grad[None], down_grad[None]


def solution(mesh):
    in_specs = (
        P("pipe", ("expert", "dp"), None),
        P(("expert", "dp"), None),
        P("pipe", ("expert", "dp"), None),
        P(("expert", "dp"), None),
        P(None, "pipe", ("expert", "dp"), None),
        P("pipe", None, ("expert", "dp"), None),
        P("pipe", None, ("expert", "dp"), None),
        P("pipe", None, ("expert", "dp"), None),
        P("pipe", "dp", "expert"),
        P("pipe", "expert", "dp"),
    )
    out_specs = (
        P(None, "pipe", ("expert", "dp"), None),
        P(None, "pipe", ("expert", "dp"), None),
        P("pipe", "dp", "expert"),
        P("pipe", "expert", "dp"),
    )
    return jax.shard_map(
        per_device, mesh=mesh, in_specs=in_specs, out_specs=out_specs, check_vma=False
    )
```

```python
import functools

import jax
import jax.numpy as jnp
import numpy as np
from jax import lax
from jax.experimental import pallas as pl
from jax.experimental.pallas import tpu as pltpu
from jax.sharding import PartitionSpec as P

MESH = pl.DeviceIdType.MESH
F32 = jnp.float32
BF16 = jnp.bfloat16
CAP = 6
QUARTERS = 4
SEMS = 312
CHUNKS = 3
ORDER = (
    ("D", 1, 2), ("D", 0, 2), ("D", 0, 1), ("D", 0, 0), ("S", 1, 2), ("D", 1, 0),
    ("S", 0, 2), ("D", 2, 0), ("S", 0, 1), ("S", 0, 0), ("S", 1, 0), ("D", 2, 1),
    ("D", 1, 1), ("D", 2, 2), ("S", 2, 0), ("G", 0, 0), ("G", 0, 1), ("G", 0, 2),
    ("D", 3, 2), ("R", 0, 0), ("S", 1, 1), ("G", 1, 0), ("G", 2, 0), ("D", 3, 0),
    ("S", 2, 1), ("S", 2, 2), ("Y", 0, 0), ("G", 1, 1), ("R", 0, 1), ("D", 3, 1),
    ("R", 0, 2), ("G", 1, 2), ("G", 2, 1), ("G", 2, 2), ("M", 0, 0), ("R", 1, 0),
    ("Y", 0, 1), ("Y", 0, 2), ("D", 4, 0), ("S", 3, 2), ("R", 1, 1), ("M", 0, 1),
    ("R", 1, 2), ("Y", 1, 0), ("Y", 1, 1), ("M", 0, 2), ("S", 4, 0), ("D", 4, 1),
    ("M", 1, 0), ("S", 3, 1), ("Y", 1, 2), ("S", 3, 0), ("D", 4, 2), ("D", 5, 0),
    ("S", 4, 1), ("M", 1, 1), ("M", 1, 2), ("S", 4, 2), ("D", 5, 1), ("D", 5, 2),
    ("S", 5, 0), ("G", 3, 0), ("G", 4, 0), ("G", 4, 1), ("G", 4, 2), ("G", 3, 1),
    ("S", 5, 1), ("S", 5, 2), ("G", 5, 0), ("R", 2, 0), ("G", 3, 2), ("G", 5, 1),
    ("G", 5, 2), ("R", 2, 1), ("R", 2, 2), ("R", 3, 0), ("Y", 2, 0), ("Y", 2, 1),
    ("Y", 2, 2), ("R", 3, 1), ("M", 2, 0), ("Y", 3, 0), ("R", 3, 2), ("Y", 3, 1),
    ("Y", 3, 2), ("M", 2, 2), ("M", 2, 1), ("WD", 0, 0), ("M", 3, 0), ("WU", 0, 0),
    ("M", 3, 1), ("M", 3, 2),
)


PASS_OF_UNIT = (0, 2, 2, 3, 1, 3)
FOLD_OF_UNIT = (0, 1, 2, 3, 4, 5)
PLACE_OF_UNIT = (4, 0, 2, 1, 5, 3)
PASS_OF_COLLECT = (0, 2, 1, 3)
KEPT_OF_COLLECT = (0, 6, 4, 7)


def regroup_matrix():
    matrix = np.zeros((192, 192), np.float32)
    for z in range(4):
        for pair in range(2):
            for half in range(2):
                for part in range(2):
                    for slot in range(CAP):
                        row = (((pair * 2 + half) * 2 + part) * 4 + z) * CAP + slot
                        column = (((z * 2 + pair) * 2 + half) * 2 + part) * CAP + slot
                        matrix[row, column] = 1.0
    return matrix


def silu_slope(values):
    logistic = jax.nn.sigmoid(values)
    return logistic * (1.0 + values * (1.0 - logistic))


def dot(left, right, dims=((1,), (0,))):
    return lax.dot_general(left, right, (dims, ((), ())), preferred_element_type=F32)


def kernel(
    sections,
    width,
    hidden,
    act_hbm,
    fresh_hbm,
    grad_hbm,
    fresh_grad_hbm,
    saved_hbm,
    up_hbm,
    down_hbm,
    place_ref,
    gate_ref,
    regroup_ref,
    regroup_back_ref,
    acts_out,
    grads_out,
    up_out,
    down_out,
    act,
    fresh,
    grad,
    fresh_grad,
    saved,
    up,
    down,
    select,
    folded,
    z_send,
    z_got,
    row_send,
    row_got,
    inputs,
    dp_send,
    dp_got,
    active_kept,
    hid_kept,
    pre_kept,
    back_send,
    back_got,
    mixed,
    relayed,
    acts_buf,
    grads_buf,
    up_buf,
    down_buf,
    send_sems,
    recv_sems,
    local_sems,
):
    half_width = 2 * width
    section = lax.axis_index("pipe")
    owner = lax.axis_index("expert")
    core = lax.axis_index("dp")
    z = owner // 4
    x = owner % 4
    pair = x // 2
    partner = z * 4 + pair * 2 + (1 - x % 2)
    across = z * 4 + (3 - x)
    diagonal = z * 4 + (x + 2) % 4
    above = ((z + 1) % 4) * 4 + x
    below = ((z + 3) % 4) * 4 + x
    opposite = ((z + 2) % 4) * 4 + x
    other = 1 - core
    ahead = (section + 1) % sections
    behind = (section + sections - 1) % sections

    loads = {}

    def load(name, source, target, index):
        loads[name] = pltpu.make_async_copy(source, target, local_sems.at[index])
        loads[name].start()

    load("act", act_hbm, act, 0)
    load("saved", saved_hbm, saved, 1)
    load("grad", grad_hbm, grad, 2)
    load("up", up_hbm, up, 3)
    load("down", down_hbm, down, 4)
    load("fresh", fresh_hbm, fresh, 5)
    load("fresh_grad", fresh_grad_hbm, fresh_grad, 6)

    barrier = pltpu.get_barrier_semaphore()
    peers = [{"dp": other}]
    for owner_there in (partner, across, diagonal):
        peers.append({"expert": owner_there})
        peers.append({"expert": owner_there, "dp": other})
    for owner_there in (above, below, opposite):
        peers.append({"expert": owner_there})
    peers += [{"pipe": ahead}, {"pipe": behind}]
    if sections == 2:
        peers = peers[:-1]
    for peer in peers:
        pl.semaphore_signal(barrier, inc=1, device_id=peer, device_id_type=MESH)

    def selection(which):
        place = place_ref[which : which + 1, :]
        expert = place >> 3
        slot = place & 7
        lane = lax.broadcasted_iota(jnp.int32, (1, 128), 1)
        z_steps = ((expert >> 1) + 4 - z) & 3
        flipped = (expert & 1) ^ pair
        row = z_steps * 48 + flipped * 24 + (lane >> 5) * CAP + slot
        rows = lax.broadcasted_iota(jnp.int32, (192, 128), 0)
        select[which] = jnp.where(rows == row, 1.0, 0.0).astype(BF16)

    def gate_column(which):
        row = gate_ref[which : which + 1, :]
        on_diagonal = lax.broadcasted_iota(jnp.int32, (128, 128), 0) == lax.broadcasted_iota(
            jnp.int32, (128, 128), 1
        )
        return jnp.sum(jnp.where(on_diagonal, row, 0.0), axis=1, keepdims=True)

    copies = []

    def remote(source, target, device):
        index = len(copies)
        copy = pltpu.make_async_remote_copy(
            src_ref=source,
            dst_ref=target,
            send_sem=send_sems.at[index],
            recv_sem=recv_sems.at[index],
            device_id=device,
            device_id_type=MESH,
        )
        copy.start()
        copies.append(copy)
        return copy

    def fold(values, slot):
        for quarter in range(QUARTERS):
            folded[slot, quarter * 32 : quarter * 32 + 32, :] = values[
                :, quarter * width : (quarter + 1) * width
            ]

    def z_start(e, lanes):
        return [
            remote(
                z_send.at[e, pl.ds(start, 48), lanes],
                z_got.at[e, pl.ds(192 - 48 - start, 48), lanes],
                {"expert": device},
            )
            for start, device in ((48, opposite), (0, above), (96, below))
        ]

    def finish(started):
        for copy in started:
            copy.wait_recv()

    def span(lanes, part):
        return pl.ds(part * width + lanes.start, lanes.size)

    def dispatch(u, which, slot, lanes):
        rows = dot(select[which], folded[slot, :, lanes]).astype(BF16)
        z_got[u, 0:48, lanes] = rows[0:48]
        z_send[u, :, lanes] = rows[48:192]
        return z_start(u, lanes)

    def spread(u, started, lanes):
        finish(started)
        rows = dot(regroup_ref[...], z_got[u, :, lanes]).astype(BF16)
        for item in range(4):
            row_send[u, item, :, lanes] = rows[48 * item : 48 * item + 48]
        row_got[u, core, :, lanes] = row_send[u, core, :, lanes]

        def to(source, target, device):
            return remote(row_send.at[u, source, :, lanes], row_got.at[u, target, :, lanes], device)

        return [
            to(2 + core, 6 + core, {"expert": diagonal}),
            to(2 + other, 6 + core, {"expert": diagonal, "dp": other}),
            to(core, 4 + core, {"expert": partner}),
            to(other, 4 + core, {"expert": partner, "dp": other}),
            to(2 + core, 2 + core, {"expert": across}),
            to(2 + other, 2 + core, {"expert": across, "dp": other}),
            to(other, core, {"dp": other}),
        ]

    def gather(u, sent, place, lanes):
        finish(sent)
        for both in range(4):
            first = row_got[u, 2 * both, :, lanes].astype(F32)
            second = row_got[u, 2 * both + 1, :, lanes].astype(F32)
            start = 192 * place + 48 * both
            for part in range(2):
                rows = jnp.concatenate(
                    [first[24 * part : 24 * part + 24], second[24 * part : 24 * part + 24]], axis=0
                )
                inputs[start : start + 48, span(lanes, part)] = rows.astype(BF16)

    def times_up(place, lanes):
        rows = pl.ds(192 * place, 192)
        return sum(
            dot(inputs[rows, span(lanes, part)], up[span(lanes, part), :]) for part in range(2)
        )

    def times_down(place, lanes):
        rows = pl.ds(192 * place, 192)
        return sum(
            dot(inputs[rows, span(lanes, part)], down[:, span(lanes, part)], ((1,), (1,)))
            for part in range(2)
        )

    def full_sum(item):
        shared[item].wait_recv()
        return dp_send[item] + dp_got[item]

    def give_back(c, product, lanes):
        parts = [product(span(lanes, part)) for part in range(2)]
        for item in (6, 7, 4, 5, 2, 3, 0, 1):
            rows = slice(24 * item, 24 * item + 24)
            back_send[c, item, :, lanes] = jnp.concatenate(
                [parts[0][rows], parts[1][rows]], axis=0
            ).astype(BF16)
        back_got[c, core, :, lanes] = back_send[c, core, :, lanes]

        def to(source, target, device):
            return remote(
                back_send.at[c, source, :, lanes], back_got.at[c, target, :, lanes], device
            )

        return [
            to(6 + core, 6 + core, {"expert": diagonal}),
            to(6 + other, 6 + core, {"expert": diagonal, "dp": other}),
            to(4 + core, 4 + core, {"expert": partner}),
            to(4 + other, 4 + core, {"expert": partner, "dp": other}),
            to(2 + core, 2 + core, {"expert": across}),
            to(2 + other, 2 + core, {"expert": across, "dp": other}),
            to(other, core, {"dp": other}),
        ]

    def returning(c, sent, lanes):
        finish(sent)
        totals = [
            (
                back_got[c, item, :, lanes].astype(F32) + back_got[c, item + 4, :, lanes].astype(F32)
            ).astype(BF16)
            for item in range(4)
        ]
        rows = dot(regroup_back_ref[...], jnp.concatenate(totals, axis=0)).astype(BF16)
        z_got[6 + c, 0:48, lanes] = rows[0:48]
        z_send[6 + c, :, lanes] = rows[48:192]
        return z_start(6 + c, lanes)

    def mix(c, which, slot, gated, started, lanes):
        finish(started)
        picked = dot(select[which], z_got[6 + c, :, lanes], ((0,), (0,)))
        if gated:
            picked = gate_column(which) * picked
        mixed[c, :, lanes] = (folded[slot, :, lanes].astype(F32) + picked).astype(BF16)

    def relay(item, device, lanes):
        return remote(mixed.at[item, :, lanes], relayed.at[item, :, lanes], {"pipe": device})

    def give_out(c, buffer, target, which, index):
        for quarter in range(QUARTERS):
            buffer[which, :, quarter * width : (quarter + 1) * width] = mixed[
                c, quarter * 32 : quarter * 32 + 32, :
            ]
        copy = pltpu.make_async_copy(buffer.at[which], target.at[which], local_sems.at[index])
        copy.start()
        return copy

    def gate_folded(which, source, target, lanes):
        folded[target, :, lanes] = (
            gate_column(which) * folded[source, :, lanes].astype(F32)
        ).astype(BF16)

    def receive(item, slot, at_end, copy, lanes):
        copy.wait_recv()
        folded[slot, :, lanes] = jnp.where(
            at_end, folded[slot, :, lanes], relayed[item, :, lanes]
        )

    groups = width // 128
    count = min(CHUNKS, groups)
    edges = [-(-groups * item // count) * 128 for item in range(count + 1)]
    chunks = [pl.ds(edges[item], edges[item + 1] - edges[item]) for item in range(count)]
    whole = pl.ds(0, width)
    last = count - 1
    weighted = {}
    shared, outputs = {}, []
    started = {}
    ready = set()

    def prepare(unit):
        if unit in ready:
            return
        ready.add(unit)
        which = PASS_OF_UNIT[unit]
        if ("select", which) not in ready:
            ready.add(("select", which))
            selection(which)
        if unit == 0:
            loads["act"].wait()
            fold(act, 0)
        elif unit == 1:
            loads["saved"].wait()
            fold(saved.at[0], 1)
        elif unit == 2:
            loads["grad"].wait()
            fold(grad, 6)
            gate_folded(2, 6, 2, whole)
        elif unit == 3:
            prepare(1)
            fold(saved.at[1], 3)
        elif unit == 4:
            loads["fresh"].wait()
            fold(fresh, 4)
        else:
            loads["fresh_grad"].wait()
            fold(fresh_grad, 7)

    def run_dispatch(unit, n, lanes):
        prepare(unit)
        if unit == 4:
            receive(0, 4, section == 0, started["relay", 0, n], lanes)
        if unit == 5:
            receive(1, 7, section == sections - 1, started["relay", 1, n], lanes)
            gate_folded(3, 7, 5, lanes)
        return dispatch(unit, PASS_OF_UNIT[unit], FOLD_OF_UNIT[unit], lanes)

    def run_spread(unit, n, lanes):
        for item in range(6):
            prepare(item)
        return spread(unit, started["D", unit, n], lanes)

    def run_gather(unit, n, lanes):
        place = PLACE_OF_UNIT[unit]
        gather(unit, started["S", unit, n], place, lanes)
        name = "down" if unit in (2, 5) else "up"
        if name not in ready:
            ready.add(name)
            loads[name].wait()
        product = times_down(place, lanes) if unit in (2, 5) else times_up(place, lanes)
        dp_send[unit] = product if n == 0 else dp_send[unit] + product
        if n == last:
            shared[unit] = remote(dp_send.at[unit], dp_got.at[unit], {"dp": other})

    def run_results(c, n, lanes):
        step = c // 2
        rows = slice(192 * step, 192 * step + 192)
        if c % 2 == 0:
            if n == 0:
                active_kept[rows] = jax.nn.silu(full_sum(4 * step)).astype(BF16)
            if "down" not in ready:
                ready.add("down")
                loads["down"].wait()
            return give_back(c, lambda columns: dot(active_kept[rows], down[:, columns]), lanes)
        if n == 0:
            projected = full_sum(1 + 2 * step)
            hid_kept[rows] = jax.nn.silu(projected).astype(BF16)
            slope = silu_slope(projected)
            pre_kept[rows] = (full_sum(2 + 3 * step) * slope).astype(BF16)
        return give_back(
            c, lambda columns: dot(pre_kept[rows], up[columns, :], ((1,), (1,))), lanes
        )

    def run_return(c, n, lanes):
        return returning(c, started["R", c, n], lanes)

    def run_mix(c, n, lanes):
        mix(c, PASS_OF_COLLECT[c], KEPT_OF_COLLECT[c], c % 2 == 0, started["Y", c, n], lanes)
        if c < 2:
            started["relay", c, n] = relay(c, ahead if c == 0 else behind, lanes)
        weighted[c] = weighted.get(c, 0) + 1
        if weighted[c] == count:
            buffer, target = ((acts_buf, acts_out), (grads_buf, grads_out))[c % 2]
            outputs.append(give_out(c, buffer, target, c // 2, 7 + c))

    def run_up_grad(unit, n, lanes):
        def up_tile(step, carry):
            start = pl.multiple_of(step * 256, 256)
            up_buf[pl.ds(start, 256), :] = dot(
                inputs[0:384, pl.ds(start, 256)], pre_kept[...], ((0,), (0,))
            ).astype(BF16)
            return carry

        lax.fori_loop(0, half_width // 256, up_tile, 0)
        outputs.append(pltpu.make_async_copy(up_buf, up_out, local_sems.at[11]))
        outputs[-1].start()

    def run_down_grad(unit, n, lanes):
        for part in range(2):
            columns = slice(part * width, (part + 1) * width)
            down_buf[:, columns] = dot(
                hid_kept[...], inputs[384:768, columns], ((0,), (0,))
            ).astype(BF16)
        outputs.append(pltpu.make_async_copy(down_buf, down_out, local_sems.at[12]))
        outputs[-1].start()

    steps = {
        "D": run_dispatch,
        "S": run_spread,
        "G": run_gather,
        "R": run_results,
        "Y": run_return,
        "M": run_mix,
        "WU": run_up_grad,
        "WD": run_down_grad,
    }
    prepare(0)
    pl.semaphore_wait(barrier, len(peers))
    for kind, unit, n in ORDER:
        started[kind, unit, n] = steps[kind](unit, n, chunks[n])
    for copy in copies:
        copy.wait_send()
    for copy in outputs:
        copy.wait()
    assert len(copies) <= SEMS


def hand_over(*refs):
    count = 4
    sources, targets, held = refs[:4], refs[4:8], refs[8:12]
    sems = refs[12]
    arrive = [
        pltpu.make_async_copy(sources[item], held[item], sems.at[item]) for item in range(count)
    ]
    leave = [
        pltpu.make_async_copy(held[item], targets[item], sems.at[count + item])
        for item in range(count)
    ]
    for copy in arrive:
        copy.start()
    for item in range(count):
        arrive[item].wait()
        leave[item].start()
    for copy in leave:
        copy.wait()


def per_device(
    act_in,
    fresh_in,
    grad_in,
    fresh_grad,
    saved_input,
    expert_ids,
    slot_ids,
    gates,
    up_weight,
    down_weight,
):
    sections = lax.axis_size("pipe")
    tokens, features = fresh_in.shape
    width = features // QUARTERS
    hidden = up_weight.shape[2]
    place = jnp.tile(expert_ids[0, :, :, 0] * 8 + slot_ids[0, :, :, 0], (1, QUARTERS))
    gate_rows = jnp.tile(gates[0, :, :, 0], (1, QUARTERS))
    regroup = regroup_matrix()
    anywhere = pl.BlockSpec(memory_space=pl.ANY)
    in_vmem = pl.BlockSpec(memory_space=pltpu.VMEM)
    full = (tokens, features)
    vm = pltpu.VMEM
    acts, grads, up_grad, down_grad = pl.pallas_call(
        functools.partial(kernel, sections, width, hidden),
        out_shape=(
            jax.ShapeDtypeStruct((2,) + full, BF16),
            jax.ShapeDtypeStruct((2,) + full, BF16),
            jax.ShapeDtypeStruct((2 * width, hidden), BF16),
            jax.ShapeDtypeStruct((hidden, 2 * width), BF16),
        ),
        in_specs=[anywhere] * 7 + [in_vmem] * 4,
        out_specs=[anywhere] * 4,
        scratch_shapes=[
            vm(full, BF16),
            vm(full, BF16),
            vm(full, BF16),
            vm(full, BF16),
            vm((2,) + full, BF16),
            vm((2 * width, hidden), BF16),
            vm((hidden, 2 * width), BF16),
            vm((4, 192, 128), BF16),
            vm((8, 128, width), BF16),
            vm((10, 144, width), BF16),
            vm((10, 192, width), BF16),
            vm((6, 4, 48, width), BF16),
            vm((6, 8, 48, width), BF16),
            vm((1152, 2 * width), BF16),
            vm((6, 192, hidden), F32),
            vm((6, 192, hidden), F32),
            vm((384, hidden), BF16),
            vm((384, hidden), BF16),
            vm((384, hidden), BF16),
            vm((4, 8, 48, width), BF16),
            vm((4, 8, 48, width), BF16),
            vm((4, 128, width), BF16),
            vm((2, 128, width), BF16),
            vm((2,) + full, BF16),
            vm((2,) + full, BF16),
            vm((2 * width, hidden), BF16),
            vm((hidden, 2 * width), BF16),
            pltpu.SemaphoreType.DMA((SEMS,)),
            pltpu.SemaphoreType.DMA((SEMS,)),
            pltpu.SemaphoreType.DMA((13,)),
        ],
        compiler_params=pltpu.CompilerParams(
            collective_id=0, has_side_effects=True, vmem_limit_bytes=60 * 2**20
        ),
    )(
        act_in[0],
        fresh_in,
        grad_in[0],
        fresh_grad,
        saved_input[:, 0],
        up_weight[0],
        down_weight[0],
        place,
        gate_rows,
        jnp.asarray(regroup, BF16),
        jnp.asarray(regroup.T, BF16),
    )
    results = (acts[:, None], grads[:, None], up_grad[None], down_grad[None])
    return pl.pallas_call(
        hand_over,
        out_shape=tuple(jax.ShapeDtypeStruct(item.shape, item.dtype) for item in results),
        in_specs=[anywhere] * 4,
        out_specs=[anywhere] * 4,
        scratch_shapes=[vm(item.shape, item.dtype) for item in results]
        + [pltpu.SemaphoreType.DMA((8,))],
        compiler_params=pltpu.CompilerParams(vmem_limit_bytes=60 * 2**20),
    )(*results)


def solution(mesh):
    in_specs = (
        P("pipe", ("expert", "dp"), None),
        P(("expert", "dp"), None),
        P("pipe", ("expert", "dp"), None),
        P(("expert", "dp"), None),
        P(None, "pipe", ("expert", "dp"), None),
        P("pipe", None, ("expert", "dp"), None),
        P("pipe", None, ("expert", "dp"), None),
        P("pipe", None, ("expert", "dp"), None),
        P("pipe", "dp", "expert"),
        P("pipe", "expert", "dp"),
    )
    out_specs = (
        P(None, "pipe", ("expert", "dp"), None),
        P(None, "pipe", ("expert", "dp"), None),
        P("pipe", "dp", "expert"),
        P("pipe", "expert", "dp"),
    )
    return jax.shard_map(
        per_device, mesh=mesh, in_specs=in_specs, out_specs=out_specs, check_vma=False
    )
```

```python
import functools

import jax
import jax.numpy as jnp
import numpy as np
from jax import lax
from jax.experimental import pallas as pl
from jax.experimental.pallas import tpu as pltpu
from jax.sharding import PartitionSpec as P

MESH = pl.DeviceIdType.MESH
F32 = jnp.float32
BF16 = jnp.bfloat16
CAP = 6
QUARTERS = 4
SEMS = 314
CHUNKS = 3
ORDER = (
    ("D", 2, 1), ("D", 2, 0), ("D", 1, 1), ("D", 2, 2), ("S", 2, 1), ("D", 0, 0),
    ("S", 2, 0), ("D", 1, 0), ("S", 1, 1), ("S", 2, 2), ("D", 1, 2), ("S", 1, 0),
    ("D", 0, 1), ("S", 0, 0), ("D", 0, 2), ("G", 2, 0), ("S", 1, 2), ("G", 1, 0),
    ("S", 0, 1), ("D", 3, 0), ("G", 2, 1), ("D", 3, 1), ("G", 2, 2), ("S", 0, 2),
    ("G", 1, 1), ("G", 1, 2), ("R", 1, 0), ("R", 1, 1), ("D", 3, 2), ("G", 0, 0),
    ("G", 0, 1), ("G", 0, 2), ("R", 1, 2), ("Y", 1, 0), ("R", 0, 0), ("Y", 1, 1),
    ("R", 0, 1), ("R", 0, 2), ("Y", 1, 2), ("Y", 0, 0), ("Y", 0, 1), ("S", 3, 0),
    ("M", 1, 0), ("M", 1, 1), ("Y", 0, 2), ("M", 0, 0), ("D", 5, 0), ("S", 3, 2),
    ("M", 1, 2), ("D", 4, 0), ("D", 5, 1), ("G", 3, 0), ("M", 0, 2), ("S", 3, 1),
    ("M", 0, 1), ("S", 5, 0), ("D", 5, 2), ("S", 4, 0), ("G", 3, 1), ("D", 4, 1),
    ("G", 3, 2), ("D", 4, 2), ("S", 5, 1), ("S", 5, 2), ("G", 5, 0), ("S", 4, 1),
    ("G", 5, 1), ("S", 4, 2), ("G", 5, 2), ("R", 3, 0), ("R", 3, 1), ("R", 3, 2),
    ("G", 4, 0), ("G", 4, 1), ("G", 4, 2), ("WD", 0, 0), ("R", 2, 0), ("Y", 3, 0),
    ("Y", 3, 1), ("R", 2, 1), ("WU", 0, 0), ("R", 2, 2), ("Y", 3, 2), ("Y", 2, 0),
    ("Y", 2, 1), ("Y", 2, 2), ("M", 3, 0), ("M", 3, 1), ("M", 2, 1), ("M", 2, 0),
    ("M", 3, 2), ("M", 2, 2),
)


PASS_OF_UNIT = (0, 2, 2, 3, 1, 3)
FOLD_OF_UNIT = (0, 1, 2, 3, 4, 5)
PLACE_OF_UNIT = (4, 0, 2, 1, 5, 3)
PASS_OF_COLLECT = (0, 2, 1, 3)
KEPT_OF_COLLECT = (0, 6, 4, 7)


def regroup_matrix():
    matrix = np.zeros((192, 192), np.float32)
    for z in range(4):
        for pair in range(2):
            for half in range(2):
                for part in range(2):
                    for slot in range(CAP):
                        row = (((pair * 2 + half) * 2 + part) * 4 + z) * CAP + slot
                        column = (((z * 2 + pair) * 2 + half) * 2 + part) * CAP + slot
                        matrix[row, column] = 1.0
    return matrix


def silu_slope(values):
    logistic = jax.nn.sigmoid(values)
    return logistic * (1.0 + values * (1.0 - logistic))


def dot(left, right, dims=((1,), (0,))):
    return lax.dot_general(left, right, (dims, ((), ())), preferred_element_type=F32)


def kernel(
    sections,
    width,
    hidden,
    act_hbm,
    fresh_hbm,
    grad_hbm,
    fresh_grad_hbm,
    saved_hbm,
    up_hbm,
    down_hbm,
    table_ref,
    regroup_ref,
    regroup_back_ref,
    acts_out,
    grads_out,
    up_out,
    down_out,
    act,
    fresh,
    grad,
    fresh_grad,
    saved,
    up,
    down,
    select,
    folded,
    z_send,
    z_got,
    row_send,
    row_got,
    inputs,
    dp_send,
    dp_got,
    active_kept,
    hid_kept,
    pre_kept,
    back_send,
    back_got,
    mixed,
    relayed,
    acts_buf,
    grads_buf,
    up_buf,
    down_buf,
    send_sems,
    recv_sems,
    local_sems,
):
    half_width = 2 * width
    section = lax.axis_index("pipe")
    owner = lax.axis_index("expert")
    core = lax.axis_index("dp")
    z = owner // 4
    x = owner % 4
    pair = x // 2
    partner = z * 4 + pair * 2 + (1 - x % 2)
    across = z * 4 + (3 - x)
    diagonal = z * 4 + (x + 2) % 4
    above = ((z + 1) % 4) * 4 + x
    below = ((z + 3) % 4) * 4 + x
    opposite = ((z + 2) % 4) * 4 + x
    other = 1 - core
    ahead = (section + 1) % sections
    behind = (section + sections - 1) % sections

    loads = {}

    def load(name, source, target, index):
        loads[name] = pltpu.make_async_copy(source, target, local_sems.at[index])
        loads[name].start()

    load("act", act_hbm, act, 0)
    load("saved", saved_hbm, saved, 1)
    load("grad", grad_hbm, grad, 2)
    load("up", up_hbm, up, 3)
    load("down", down_hbm, down, 4)
    load("fresh", fresh_hbm, fresh, 5)
    load("fresh_grad", fresh_grad_hbm, fresh_grad, 6)

    barrier = pltpu.get_barrier_semaphore()
    peers = [{"dp": other}]
    for owner_there in (partner, across, diagonal):
        peers.append({"expert": owner_there})
        peers.append({"expert": owner_there, "dp": other})
    for owner_there in (above, below, opposite):
        peers.append({"expert": owner_there})
    peers += [{"pipe": ahead}, {"pipe": behind}]
    if sections == 2:
        peers = peers[:-1]
    for peer in peers:
        pl.semaphore_signal(barrier, inc=1, device_id=peer, device_id_type=MESH)

    def selection(which):
        row = table_ref[which : which + 1, :]
        place = jnp.concatenate([row] * QUARTERS, axis=1).astype(jnp.int32)
        expert = place >> 3
        slot = place & 7
        lane = lax.broadcasted_iota(jnp.int32, (1, 128), 1)
        z_steps = ((expert >> 1) + 4 - z) & 3
        flipped = (expert & 1) ^ pair
        row = z_steps * 48 + flipped * 24 + (lane >> 5) * CAP + slot
        rows = lax.broadcasted_iota(jnp.int32, (192, 128), 0)
        select[which] = jnp.where(rows == row, 1.0, 0.0).astype(BF16)

    def gate_column(which):
        row = jnp.concatenate([table_ref[4 + which : 5 + which, :]] * QUARTERS, axis=1)
        on_diagonal = lax.broadcasted_iota(jnp.int32, (128, 128), 0) == lax.broadcasted_iota(
            jnp.int32, (128, 128), 1
        )
        return jnp.sum(jnp.where(on_diagonal, row, 0.0), axis=1, keepdims=True)

    copies = []
    relays = {}

    def remote(source, target, device):
        index = len(copies)
        copy = pltpu.make_async_remote_copy(
            src_ref=source,
            dst_ref=target,
            send_sem=send_sems.at[index],
            recv_sem=recv_sems.at[index],
            device_id=device,
            device_id_type=MESH,
        )
        copy.start()
        copies.append(copy)
        return copy

    def fold(values, slot):
        for quarter in range(QUARTERS):
            folded[slot, quarter * 32 : quarter * 32 + 32, :] = values[
                :, quarter * width : (quarter + 1) * width
            ]

    def z_start(e, lanes):
        return [
            remote(
                z_send.at[e, pl.ds(start, 48), lanes],
                z_got.at[e, pl.ds(192 - 48 - start, 48), lanes],
                {"expert": device},
            )
            for start, device in ((48, opposite), (0, above), (96, below))
        ]

    def finish(started):
        for copy in started:
            copy.wait_recv()

    def span(lanes, part):
        return pl.ds(part * width + lanes.start, lanes.size)

    def dispatch(u, which, slot, lanes):
        rows = dot(select[which], folded[slot, :, lanes]).astype(BF16)
        z_got[u, 0:48, lanes] = rows[0:48]
        z_send[u, :, lanes] = rows[48:192]
        return z_start(u, lanes)

    def spread(u, started, lanes):
        finish(started)
        rows = dot(regroup_ref[...], z_got[u, :, lanes]).astype(BF16)
        for item in range(4):
            row_send[u, item, :, lanes] = rows[48 * item : 48 * item + 48]
        row_got[u, core, :, lanes] = row_send[u, core, :, lanes]

        def to(source, target, device):
            return remote(row_send.at[u, source, :, lanes], row_got.at[u, target, :, lanes], device)

        return [
            to(2 + core, 6 + core, {"expert": diagonal}),
            to(2 + other, 6 + core, {"expert": diagonal, "dp": other}),
            to(core, 4 + core, {"expert": partner}),
            to(other, 4 + core, {"expert": partner, "dp": other}),
            to(2 + core, 2 + core, {"expert": across}),
            to(2 + other, 2 + core, {"expert": across, "dp": other}),
            to(other, core, {"dp": other}),
        ]

    def gather(u, sent, place, lanes):
        finish(sent)
        for both in range(4):
            first = row_got[u, 2 * both, :, lanes].astype(F32)
            second = row_got[u, 2 * both + 1, :, lanes].astype(F32)
            start = 192 * place + 48 * both
            for part in range(2):
                rows = jnp.concatenate(
                    [first[24 * part : 24 * part + 24], second[24 * part : 24 * part + 24]], axis=0
                )
                inputs[start : start + 48, span(lanes, part)] = rows.astype(BF16)

    def times_up(place, lanes):
        rows = pl.ds(192 * place, 192)
        return sum(
            dot(inputs[rows, span(lanes, part)], up[span(lanes, part), :]) for part in range(2)
        )

    def times_down(place, lanes):
        rows = pl.ds(192 * place, 192)
        return sum(
            dot(inputs[rows, span(lanes, part)], down[:, span(lanes, part)], ((1,), (1,)))
            for part in range(2)
        )

    def full_sum(item):
        shared[item].wait_recv()
        return dp_send[item] + dp_got[item]

    def give_back(c, product, lanes):
        parts = [product(span(lanes, part)) for part in range(2)]
        for item in (6, 7, 4, 5, 2, 3, 0, 1):
            rows = slice(24 * item, 24 * item + 24)
            back_send[c, item, :, lanes] = jnp.concatenate(
                [parts[0][rows], parts[1][rows]], axis=0
            ).astype(BF16)
        back_got[c, core, :, lanes] = back_send[c, core, :, lanes]

        def to(source, target, device):
            return remote(
                back_send.at[c, source, :, lanes], back_got.at[c, target, :, lanes], device
            )

        return [
            to(6 + core, 6 + core, {"expert": diagonal}),
            to(6 + other, 6 + core, {"expert": diagonal, "dp": other}),
            to(4 + core, 4 + core, {"expert": partner}),
            to(4 + other, 4 + core, {"expert": partner, "dp": other}),
            to(2 + core, 2 + core, {"expert": across}),
            to(2 + other, 2 + core, {"expert": across, "dp": other}),
            to(other, core, {"dp": other}),
        ]

    def returning(c, sent, lanes):
        finish(sent)
        totals = [
            (
                back_got[c, item, :, lanes].astype(F32) + back_got[c, item + 4, :, lanes].astype(F32)
            ).astype(BF16)
            for item in range(4)
        ]
        rows = dot(regroup_back_ref[...], jnp.concatenate(totals, axis=0)).astype(BF16)
        z_got[6 + c, 0:48, lanes] = rows[0:48]
        z_send[6 + c, :, lanes] = rows[48:192]
        return z_start(6 + c, lanes)

    def mix(c, which, slot, gated, started, lanes):
        finish(started)
        picked = dot(select[which], z_got[6 + c, :, lanes], ((0,), (0,)))
        if gated:
            picked = gate_column(which) * picked
        mixed[c, :, lanes] = (folded[slot, :, lanes].astype(F32) + picked).astype(BF16)

    def relay(item, device, sends, lanes):
        index = len(copies)
        copy = pltpu.make_async_remote_copy(
            src_ref=mixed.at[item, :, lanes],
            dst_ref=relayed.at[item, :, lanes],
            send_sem=send_sems.at[index],
            recv_sem=recv_sems.at[index],
            device_id={"pipe": device},
            device_id_type=MESH,
        )
        pl.when(sends)(copy.start)
        copies.append(copy)
        relays[index] = sends
        return copy

    def give_out(c, buffer, target, which, index):
        for quarter in range(QUARTERS):
            buffer[which, :, quarter * width : (quarter + 1) * width] = mixed[
                c, quarter * 32 : quarter * 32 + 32, :
            ]
        copy = pltpu.make_async_copy(buffer.at[which], target.at[which], local_sems.at[index])
        copy.start()
        return copy

    def gate_folded(which, source, target, lanes):
        folded[target, :, lanes] = (
            gate_column(which) * folded[source, :, lanes].astype(F32)
        ).astype(BF16)

    def receive(item, slot, at_end, copy, lanes):
        @pl.when(jnp.logical_not(at_end))
        def _():
            copy.wait_recv()
            folded[slot, :, lanes] = relayed[item, :, lanes]

    groups = width // 128
    count = min(CHUNKS, groups)
    edges = [groups * item // count * 128 for item in range(count + 1)]
    chunks = [pl.ds(edges[item], edges[item + 1] - edges[item]) for item in range(count)]
    whole = pl.ds(0, width)
    last = count - 1
    weighted = {}
    shared, outputs = {}, []
    started = {}
    ready = set()

    def prepare(unit):
        if unit in ready:
            return
        ready.add(unit)
        which = PASS_OF_UNIT[unit]
        if ("select", which) not in ready:
            ready.add(("select", which))
            selection(which)
        if unit == 0:
            loads["act"].wait()
            fold(act, 0)
        elif unit == 1:
            loads["saved"].wait()
            fold(saved.at[0], 1)
        elif unit == 2:
            loads["grad"].wait()
            fold(grad, 6)
            gate_folded(2, 6, 2, whole)
        elif unit == 3:
            prepare(1)
            fold(saved.at[1], 3)
        elif unit == 4:
            loads["fresh"].wait()
            fold(fresh, 4)
        else:
            loads["fresh_grad"].wait()
            fold(fresh_grad, 7)

    def run_dispatch(unit, n, lanes):
        prepare(unit)
        if unit == 4:
            receive(0, 4, section == 0, started["relay", 0, n], lanes)
        if unit == 5:
            receive(1, 7, section == sections - 1, started["relay", 1, n], lanes)
            gate_folded(3, 7, 5, lanes)
        return dispatch(unit, PASS_OF_UNIT[unit], FOLD_OF_UNIT[unit], lanes)

    def run_spread(unit, n, lanes):
        for item in range(6):
            prepare(item)
        return spread(unit, started["D", unit, n], lanes)

    def run_gather(unit, n, lanes):
        place = PLACE_OF_UNIT[unit]
        gather(unit, started["S", unit, n], place, lanes)
        name = "down" if unit in (2, 5) else "up"
        if name not in ready:
            ready.add(name)
            loads[name].wait()
        product = times_down(place, lanes) if unit in (2, 5) else times_up(place, lanes)
        dp_send[unit] = product if n == 0 else dp_send[unit] + product
        if n == last:
            shared[unit] = remote(dp_send.at[unit], dp_got.at[unit], {"dp": other})

    def run_results(c, n, lanes):
        step = c // 2
        rows = slice(192 * step, 192 * step + 192)
        if c % 2 == 0:
            if n == 0:
                active_kept[rows] = jax.nn.silu(full_sum(4 * step)).astype(BF16)
            if "down" not in ready:
                ready.add("down")
                loads["down"].wait()
            return give_back(c, lambda columns: dot(active_kept[rows], down[:, columns]), lanes)
        if n == 0:
            projected = full_sum(1 + 2 * step)
            hid_kept[rows] = jax.nn.silu(projected).astype(BF16)
            slope = silu_slope(projected)
            pre_kept[rows] = (full_sum(2 + 3 * step) * slope).astype(BF16)
        return give_back(
            c, lambda columns: dot(pre_kept[rows], up[columns, :], ((1,), (1,))), lanes
        )

    def run_return(c, n, lanes):
        return returning(c, started["R", c, n], lanes)

    def run_mix(c, n, lanes):
        mix(c, PASS_OF_COLLECT[c], KEPT_OF_COLLECT[c], c % 2 == 0, started["Y", c, n], lanes)
        if c < 2:
            device = ahead if c == 0 else behind
            sends = section < sections - 1 if c == 0 else section > 0
            started["relay", c, n] = relay(c, device, sends, lanes)
        weighted[c] = weighted.get(c, 0) + 1
        if weighted[c] == count:
            buffer, target = ((acts_buf, acts_out), (grads_buf, grads_out))[c % 2]
            outputs.append(give_out(c, buffer, target, c // 2, 7 + c))

    def run_up_grad(unit, n, lanes):
        def up_tile(step, carry):
            start = pl.multiple_of(step * 256, 256)
            up_buf[pl.ds(start, 256), :] = dot(
                inputs[0:384, pl.ds(start, 256)], pre_kept[...], ((0,), (0,))
            ).astype(BF16)
            return carry

        lax.fori_loop(0, half_width // 256, up_tile, 0)
        outputs.append(pltpu.make_async_copy(up_buf, up_out, local_sems.at[11]))
        outputs[-1].start()

    def run_down_grad(unit, n, lanes):
        for part in range(2):
            columns = slice(part * width, (part + 1) * width)
            down_buf[:, columns] = dot(
                hid_kept[...], inputs[384:768, columns], ((0,), (0,))
            ).astype(BF16)
        outputs.append(pltpu.make_async_copy(down_buf, down_out, local_sems.at[12]))
        outputs[-1].start()

    steps = {
        "D": run_dispatch,
        "S": run_spread,
        "G": run_gather,
        "R": run_results,
        "Y": run_return,
        "M": run_mix,
        "WU": run_up_grad,
        "WD": run_down_grad,
    }
    prepare(0)
    pl.semaphore_wait(barrier, len(peers))
    for kind, unit, n in ORDER:
        started[kind, unit, n] = steps[kind](unit, n, chunks[n])
    for index, copy in enumerate(copies):
        if index in relays:
            pl.when(relays[index])(copy.wait_send)
        else:
            copy.wait_send()
    for copy in outputs:
        copy.wait()
    assert len(copies) <= SEMS


def hand_over(*refs):
    count = 4
    sources, targets, held = refs[:4], refs[4:8], refs[8:12]
    sems = refs[12]
    arrive = [
        pltpu.make_async_copy(sources[item], held[item], sems.at[item]) for item in range(count)
    ]
    leave = [
        pltpu.make_async_copy(held[item], targets[item], sems.at[count + item])
        for item in range(count)
    ]
    for copy in arrive:
        copy.start()
    for item in range(count):
        arrive[item].wait()
        leave[item].start()
    for copy in leave:
        copy.wait()


def per_device(
    act_in,
    fresh_in,
    grad_in,
    fresh_grad,
    saved_input,
    expert_ids,
    slot_ids,
    gates,
    up_weight,
    down_weight,
):
    sections = lax.axis_size("pipe")
    tokens, features = fresh_in.shape
    width = features // QUARTERS
    hidden = up_weight.shape[2]
    place = (expert_ids * 8 + slot_ids).astype(F32)
    table = jnp.concatenate([place, gates], axis=1).reshape(8, tokens)
    regroup = regroup_matrix()
    anywhere = pl.BlockSpec(memory_space=pl.ANY)
    in_vmem = pl.BlockSpec(memory_space=pltpu.VMEM)
    full = (tokens, features)
    vm = pltpu.VMEM
    acts, grads, up_grad, down_grad = pl.pallas_call(
        functools.partial(kernel, sections, width, hidden),
        out_shape=(
            jax.ShapeDtypeStruct((2,) + full, BF16),
            jax.ShapeDtypeStruct((2,) + full, BF16),
            jax.ShapeDtypeStruct((2 * width, hidden), BF16),
            jax.ShapeDtypeStruct((hidden, 2 * width), BF16),
        ),
        in_specs=[anywhere] * 7 + [in_vmem] * 3,
        out_specs=[anywhere] * 4,
        scratch_shapes=[
            vm(full, BF16),
            vm(full, BF16),
            vm(full, BF16),
            vm(full, BF16),
            vm((2,) + full, BF16),
            vm((2 * width, hidden), BF16),
            vm((hidden, 2 * width), BF16),
            vm((4, 192, 128), BF16),
            vm((8, 128, width), BF16),
            vm((10, 144, width), BF16),
            vm((10, 192, width), BF16),
            vm((6, 4, 48, width), BF16),
            vm((6, 8, 48, width), BF16),
            vm((1152, 2 * width), BF16),
            vm((6, 192, hidden), F32),
            vm((6, 192, hidden), F32),
            vm((384, hidden), BF16),
            vm((384, hidden), BF16),
            vm((384, hidden), BF16),
            vm((4, 8, 48, width), BF16),
            vm((4, 8, 48, width), BF16),
            vm((4, 128, width), BF16),
            vm((2, 128, width), BF16),
            vm((2,) + full, BF16),
            vm((2,) + full, BF16),
            vm((2 * width, hidden), BF16),
            vm((hidden, 2 * width), BF16),
            pltpu.SemaphoreType.DMA((SEMS,)),
            pltpu.SemaphoreType.DMA((SEMS,)),
            pltpu.SemaphoreType.DMA((13,)),
        ],
        compiler_params=pltpu.CompilerParams(
            collective_id=0, has_side_effects=True, vmem_limit_bytes=60 * 2**20
        ),
    )(
        act_in[0],
        fresh_in,
        grad_in[0],
        fresh_grad,
        saved_input[:, 0],
        up_weight[0],
        down_weight[0],
        table,
        jnp.asarray(regroup, BF16),
        jnp.asarray(regroup.T, BF16),
    )
    results = (acts[:, None], grads[:, None], up_grad[None], down_grad[None])
    return pl.pallas_call(
        hand_over,
        out_shape=tuple(jax.ShapeDtypeStruct(item.shape, item.dtype) for item in results),
        in_specs=[anywhere] * 4,
        out_specs=[anywhere] * 4,
        scratch_shapes=[vm(item.shape, item.dtype) for item in results]
        + [pltpu.SemaphoreType.DMA((8,))],
        compiler_params=pltpu.CompilerParams(vmem_limit_bytes=60 * 2**20),
    )(*results)


def solution(mesh):
    in_specs = (
        P("pipe", ("expert", "dp"), None),
        P(("expert", "dp"), None),
        P("pipe", ("expert", "dp"), None),
        P(("expert", "dp"), None),
        P(None, "pipe", ("expert", "dp"), None),
        P("pipe", None, ("expert", "dp"), None),
        P("pipe", None, ("expert", "dp"), None),
        P("pipe", None, ("expert", "dp"), None),
        P("pipe", "dp", "expert"),
        P("pipe", "expert", "dp"),
    )
    out_specs = (
        P(None, "pipe", ("expert", "dp"), None),
        P(None, "pipe", ("expert", "dp"), None),
        P("pipe", "dp", "expert"),
        P("pipe", "expert", "dp"),
    )
    return jax.shard_map(
        per_device, mesh=mesh, in_specs=in_specs, out_specs=out_specs, check_vma=False
    )
```

```python
import functools

import jax
import jax.numpy as jnp
import numpy as np
from jax import lax
from jax.experimental import pallas as pl
from jax.experimental.pallas import tpu as pltpu
from jax.sharding import PartitionSpec as P

MESH = pl.DeviceIdType.MESH
F32 = jnp.float32
BF16 = jnp.bfloat16
CAP = 6
QUARTERS = 4
SEMS = 314
CHUNKS = 3
ORDER = (
    ("D", 2, 1), ("D", 2, 0), ("D", 1, 1), ("D", 2, 2), ("S", 2, 1), ("D", 0, 0),
    ("S", 2, 0), ("D", 1, 0), ("S", 1, 1), ("S", 2, 2), ("D", 1, 2), ("S", 1, 0),
    ("D", 0, 1), ("S", 0, 0), ("D", 0, 2), ("G", 2, 0), ("S", 1, 2), ("G", 1, 0),
    ("S", 0, 1), ("D", 3, 0), ("G", 2, 1), ("D", 3, 1), ("G", 2, 2), ("S", 0, 2),
    ("G", 1, 1), ("G", 1, 2), ("R", 1, 0), ("R", 1, 1), ("D", 3, 2), ("G", 0, 0),
    ("G", 0, 1), ("G", 0, 2), ("R", 1, 2), ("Y", 1, 0), ("R", 0, 0), ("Y", 1, 1),
    ("R", 0, 1), ("R", 0, 2), ("Y", 1, 2), ("Y", 0, 0), ("Y", 0, 1), ("S", 3, 0),
    ("M", 1, 0), ("M", 1, 1), ("Y", 0, 2), ("M", 0, 0), ("D", 5, 0), ("S", 3, 2),
    ("M", 1, 2), ("D", 4, 0), ("D", 5, 1), ("G", 3, 0), ("M", 0, 2), ("S", 3, 1),
    ("M", 0, 1), ("S", 5, 0), ("D", 5, 2), ("S", 4, 0), ("G", 3, 1), ("D", 4, 1),
    ("G", 3, 2), ("D", 4, 2), ("S", 5, 1), ("S", 5, 2), ("G", 5, 0), ("S", 4, 1),
    ("G", 5, 1), ("S", 4, 2), ("G", 5, 2), ("R", 3, 0), ("R", 3, 1), ("R", 3, 2),
    ("G", 4, 0), ("G", 4, 1), ("G", 4, 2), ("WD", 0, 0), ("R", 2, 0), ("Y", 3, 0),
    ("Y", 3, 1), ("R", 2, 1), ("WU", 0, 0), ("R", 2, 2), ("Y", 3, 2), ("Y", 2, 0),
    ("Y", 2, 1), ("Y", 2, 2), ("M", 3, 0), ("M", 3, 1), ("M", 2, 1), ("M", 2, 0),
    ("M", 3, 2), ("M", 2, 2),
)


PASS_OF_UNIT = (0, 2, 2, 3, 1, 3)
FOLD_OF_UNIT = (0, 1, 2, 3, 4, 5)
PLACE_OF_UNIT = (4, 0, 2, 1, 5, 3)
PASS_OF_COLLECT = (0, 2, 1, 3)
KEPT_OF_COLLECT = (0, 6, 4, 7)


def regroup_matrix():
    matrix = np.zeros((192, 192), np.float32)
    for z in range(4):
        for pair in range(2):
            for half in range(2):
                for part in range(2):
                    for slot in range(CAP):
                        row = (((pair * 2 + half) * 2 + part) * 4 + z) * CAP + slot
                        column = (((z * 2 + pair) * 2 + half) * 2 + part) * CAP + slot
                        matrix[row, column] = 1.0
    return matrix


def silu_slope(values):
    logistic = jax.nn.sigmoid(values)
    return logistic * (1.0 + values * (1.0 - logistic))


def dot(left, right, dims=((1,), (0,))):
    return lax.dot_general(left, right, (dims, ((), ())), preferred_element_type=F32)


def kernel(
    sections,
    width,
    hidden,
    act_hbm,
    fresh_hbm,
    grad_hbm,
    fresh_grad_hbm,
    saved_hbm,
    up_hbm,
    down_hbm,
    table_ref,
    regroup_ref,
    regroup_back_ref,
    acts_out,
    grads_out,
    up_out,
    down_out,
    act,
    fresh,
    grad,
    fresh_grad,
    saved,
    up,
    down,
    select,
    folded,
    z_send,
    z_got,
    row_send,
    row_got,
    inputs,
    dp_send,
    dp_got,
    active_kept,
    hid_kept,
    pre_kept,
    back_send,
    back_got,
    mixed,
    relayed,
    acts_buf,
    grads_buf,
    up_buf,
    down_buf,
    send_sems,
    recv_sems,
    local_sems,
):
    half_width = 2 * width
    section = lax.axis_index("pipe")
    owner = lax.axis_index("expert")
    core = lax.axis_index("dp")
    z = owner // 4
    x = owner % 4
    pair = x // 2
    partner = z * 4 + pair * 2 + (1 - x % 2)
    across = z * 4 + (3 - x)
    diagonal = z * 4 + (x + 2) % 4
    above = ((z + 1) % 4) * 4 + x
    below = ((z + 3) % 4) * 4 + x
    opposite = ((z + 2) % 4) * 4 + x
    other = 1 - core
    ahead = (section + 1) % sections
    behind = (section + sections - 1) % sections

    loads = {}

    def load(name, source, target, index):
        loads[name] = pltpu.make_async_copy(source, target, local_sems.at[index])
        loads[name].start()

    load("act", act_hbm, act, 0)
    load("saved", saved_hbm, saved, 1)
    load("grad", grad_hbm, grad, 2)
    load("up", up_hbm, up, 3)
    load("down", down_hbm, down, 4)
    load("fresh", fresh_hbm, fresh, 5)
    load("fresh_grad", fresh_grad_hbm, fresh_grad, 6)

    barrier = pltpu.get_barrier_semaphore()
    peers = [{"dp": other}]
    for owner_there in (partner, across, diagonal):
        peers.append({"expert": owner_there})
        peers.append({"expert": owner_there, "dp": other})
    for owner_there in (above, below, opposite):
        peers.append({"expert": owner_there})
    peers += [{"pipe": ahead}, {"pipe": behind}]
    if sections == 2:
        peers = peers[:-1]
    for peer in peers:
        pl.semaphore_signal(barrier, inc=1, device_id=peer, device_id_type=MESH)

    def selection(which):
        row = table_ref[which : which + 1, :]
        place = jnp.concatenate([row] * QUARTERS, axis=1).astype(jnp.int32)
        expert = place >> 3
        slot = place & 7
        lane = lax.broadcasted_iota(jnp.int32, (1, 128), 1)
        z_steps = ((expert >> 1) + 4 - z) & 3
        flipped = (expert & 1) ^ pair
        row = z_steps * 48 + flipped * 24 + (lane >> 5) * CAP + slot
        rows = lax.broadcasted_iota(jnp.int32, (192, 128), 0)
        select[which] = jnp.where(rows == row, 1.0, 0.0).astype(BF16)

    def gate_column(which):
        row = jnp.concatenate([table_ref[4 + which : 5 + which, :]] * QUARTERS, axis=1)
        on_diagonal = lax.broadcasted_iota(jnp.int32, (128, 128), 0) == lax.broadcasted_iota(
            jnp.int32, (128, 128), 1
        )
        return jnp.sum(jnp.where(on_diagonal, row, 0.0), axis=1, keepdims=True)

    copies = []
    relays = {}

    def remote(source, target, device):
        index = len(copies)
        copy = pltpu.make_async_remote_copy(
            src_ref=source,
            dst_ref=target,
            send_sem=send_sems.at[index],
            recv_sem=recv_sems.at[index],
            device_id=device,
            device_id_type=MESH,
        )
        copy.start()
        copies.append(copy)
        return copy

    def fold(values, slot):
        for quarter in range(QUARTERS):
            folded[slot, quarter * 32 : quarter * 32 + 32, :] = values[
                :, quarter * width : (quarter + 1) * width
            ]

    def z_start(e, lanes):
        return [
            remote(
                z_send.at[e, pl.ds(start, 48), lanes],
                z_got.at[e, pl.ds(192 - 48 - start, 48), lanes],
                {"expert": device},
            )
            for start, device in ((48, opposite), (0, above), (96, below))
        ]

    def finish(started):
        for copy in started:
            copy.wait_recv()

    def span(lanes, part):
        return pl.ds(part * width + lanes.start, lanes.size)

    def dispatch(u, which, slot, lanes):
        rows = dot(select[which], folded[slot, :, lanes]).astype(BF16)
        z_got[u, 0:48, lanes] = rows[0:48]
        z_send[u, :, lanes] = rows[48:192]
        if not copies:
            pl.semaphore_wait(barrier, len(peers))
        return z_start(u, lanes)

    def spread(u, started, lanes):
        finish(started)
        rows = dot(regroup_ref[...], z_got[u, :, lanes]).astype(BF16)
        for item in range(4):
            row_send[u, item, :, lanes] = rows[48 * item : 48 * item + 48]
        row_got[u, core, :, lanes] = row_send[u, core, :, lanes]

        def to(source, target, device):
            return remote(row_send.at[u, source, :, lanes], row_got.at[u, target, :, lanes], device)

        return [
            to(2 + core, 6 + core, {"expert": diagonal}),
            to(2 + other, 6 + core, {"expert": diagonal, "dp": other}),
            to(core, 4 + core, {"expert": partner}),
            to(other, 4 + core, {"expert": partner, "dp": other}),
            to(2 + core, 2 + core, {"expert": across}),
            to(2 + other, 2 + core, {"expert": across, "dp": other}),
            to(other, core, {"dp": other}),
        ]

    def gather(u, sent, place, lanes):
        finish(sent)
        for both in range(4):
            first = row_got[u, 2 * both, :, lanes].astype(F32)
            second = row_got[u, 2 * both + 1, :, lanes].astype(F32)
            start = 192 * place + 48 * both
            for part in range(2):
                rows = jnp.concatenate(
                    [first[24 * part : 24 * part + 24], second[24 * part : 24 * part + 24]], axis=0
                )
                inputs[start : start + 48, span(lanes, part)] = rows.astype(BF16)

    def times_up(place, lanes):
        rows = pl.ds(192 * place, 192)
        return sum(
            dot(inputs[rows, span(lanes, part)], up[span(lanes, part), :]) for part in range(2)
        )

    def times_down(place, lanes):
        rows = pl.ds(192 * place, 192)
        return sum(
            dot(inputs[rows, span(lanes, part)], down[:, span(lanes, part)], ((1,), (1,)))
            for part in range(2)
        )

    def full_sum(item):
        shared[item].wait_recv()
        return dp_send[item] + dp_got[item]

    def give_back(c, product, lanes):
        parts = [product(span(lanes, part)) for part in range(2)]
        for item in (6, 7, 4, 5, 2, 3, 0, 1):
            rows = slice(24 * item, 24 * item + 24)
            back_send[c, item, :, lanes] = jnp.concatenate(
                [parts[0][rows], parts[1][rows]], axis=0
            ).astype(BF16)
        back_got[c, core, :, lanes] = back_send[c, core, :, lanes]

        def to(source, target, device):
            return remote(
                back_send.at[c, source, :, lanes], back_got.at[c, target, :, lanes], device
            )

        return [
            to(6 + core, 6 + core, {"expert": diagonal}),
            to(6 + other, 6 + core, {"expert": diagonal, "dp": other}),
            to(4 + core, 4 + core, {"expert": partner}),
            to(4 + other, 4 + core, {"expert": partner, "dp": other}),
            to(2 + core, 2 + core, {"expert": across}),
            to(2 + other, 2 + core, {"expert": across, "dp": other}),
            to(other, core, {"dp": other}),
        ]

    def returning(c, sent, lanes):
        finish(sent)
        totals = [
            (
                back_got[c, item, :, lanes].astype(F32) + back_got[c, item + 4, :, lanes].astype(F32)
            ).astype(BF16)
            for item in range(4)
        ]
        rows = dot(regroup_back_ref[...], jnp.concatenate(totals, axis=0)).astype(BF16)
        z_got[6 + c, 0:48, lanes] = rows[0:48]
        z_send[6 + c, :, lanes] = rows[48:192]
        return z_start(6 + c, lanes)

    def mix(c, which, slot, gated, started, lanes):
        finish(started)
        picked = dot(select[which], z_got[6 + c, :, lanes], ((0,), (0,)))
        if gated:
            picked = gate_column(which) * picked
        mixed[c, :, lanes] = (folded[slot, :, lanes].astype(F32) + picked).astype(BF16)

    def relay(item, device, sends, lanes):
        index = len(copies)
        copy = pltpu.make_async_remote_copy(
            src_ref=mixed.at[item, :, lanes],
            dst_ref=relayed.at[item, :, lanes],
            send_sem=send_sems.at[index],
            recv_sem=recv_sems.at[index],
            device_id={"pipe": device},
            device_id_type=MESH,
        )
        pl.when(sends)(copy.start)
        copies.append(copy)
        relays[index] = sends
        return copy

    def give_out(c, buffer, target, which, index):
        for quarter in range(QUARTERS):
            buffer[which, :, quarter * width : (quarter + 1) * width] = mixed[
                c, quarter * 32 : quarter * 32 + 32, :
            ]
        copy = pltpu.make_async_copy(buffer.at[which], target.at[which], local_sems.at[index])
        copy.start()
        return copy

    def gate_folded(which, source, target, lanes):
        folded[target, :, lanes] = (
            gate_column(which) * folded[source, :, lanes].astype(F32)
        ).astype(BF16)

    def receive(item, slot, at_end, copy, lanes):
        @pl.when(jnp.logical_not(at_end))
        def _():
            copy.wait_recv()
            folded[slot, :, lanes] = relayed[item, :, lanes]

    groups = width // 128
    count = min(CHUNKS, groups)
    edges = [groups * item // count * 128 for item in range(count + 1)]
    chunks = [pl.ds(edges[item], edges[item + 1] - edges[item]) for item in range(count)]
    whole = pl.ds(0, width)
    last = count - 1
    weighted = {}
    shared, outputs = {}, []
    started = {}
    ready = set()

    def prepare(unit):
        if unit in ready:
            return
        ready.add(unit)
        which = PASS_OF_UNIT[unit]
        if ("select", which) not in ready:
            ready.add(("select", which))
            selection(which)
        if unit == 0:
            loads["act"].wait()
            fold(act, 0)
        elif unit == 1:
            loads["saved"].wait()
            fold(saved.at[0], 1)
        elif unit == 2:
            loads["grad"].wait()
            fold(grad, 6)
            gate_folded(2, 6, 2, whole)
        elif unit == 3:
            prepare(1)
            fold(saved.at[1], 3)
        elif unit == 4:
            loads["fresh"].wait()
            fold(fresh, 4)
        else:
            loads["fresh_grad"].wait()
            fold(fresh_grad, 7)

    def run_dispatch(unit, n, lanes):
        prepare(unit)
        if unit == 4:
            receive(0, 4, section == 0, started["relay", 0, n], lanes)
        if unit == 5:
            receive(1, 7, section == sections - 1, started["relay", 1, n], lanes)
            gate_folded(3, 7, 5, lanes)
        return dispatch(unit, PASS_OF_UNIT[unit], FOLD_OF_UNIT[unit], lanes)

    def run_spread(unit, n, lanes):
        for item in range(6):
            prepare(item)
        return spread(unit, started["D", unit, n], lanes)

    def run_gather(unit, n, lanes):
        place = PLACE_OF_UNIT[unit]
        gather(unit, started["S", unit, n], place, lanes)
        name = "down" if unit in (2, 5) else "up"
        if name not in ready:
            ready.add(name)
            loads[name].wait()
        product = times_down(place, lanes) if unit in (2, 5) else times_up(place, lanes)
        dp_send[unit] = product if n == 0 else dp_send[unit] + product
        if n == last:
            shared[unit] = remote(dp_send.at[unit], dp_got.at[unit], {"dp": other})

    def run_results(c, n, lanes):
        step = c // 2
        rows = slice(192 * step, 192 * step + 192)
        if c % 2 == 0:
            if n == 0:
                active_kept[rows] = jax.nn.silu(full_sum(4 * step)).astype(BF16)
            if "down" not in ready:
                ready.add("down")
                loads["down"].wait()
            return give_back(c, lambda columns: dot(active_kept[rows], down[:, columns]), lanes)
        if n == 0:
            projected = full_sum(1 + 2 * step)
            hid_kept[rows] = jax.nn.silu(projected).astype(BF16)
            slope = silu_slope(projected)
            pre_kept[rows] = (full_sum(2 + 3 * step) * slope).astype(BF16)
        return give_back(
            c, lambda columns: dot(pre_kept[rows], up[columns, :], ((1,), (1,))), lanes
        )

    def run_return(c, n, lanes):
        return returning(c, started["R", c, n], lanes)

    def run_mix(c, n, lanes):
        mix(c, PASS_OF_COLLECT[c], KEPT_OF_COLLECT[c], c % 2 == 0, started["Y", c, n], lanes)
        if c < 2:
            device = ahead if c == 0 else behind
            sends = section < sections - 1 if c == 0 else section > 0
            started["relay", c, n] = relay(c, device, sends, lanes)
        weighted[c] = weighted.get(c, 0) + 1
        if weighted[c] == count:
            buffer, target = ((acts_buf, acts_out), (grads_buf, grads_out))[c % 2]
            outputs.append(give_out(c, buffer, target, c // 2, 7 + c))

    def run_up_grad(unit, n, lanes):
        def up_tile(step, carry):
            start = pl.multiple_of(step * 256, 256)
            up_buf[pl.ds(start, 256), :] = dot(
                inputs[0:384, pl.ds(start, 256)], pre_kept[...], ((0,), (0,))
            ).astype(BF16)
            return carry

        lax.fori_loop(0, half_width // 256, up_tile, 0)
        outputs.append(pltpu.make_async_copy(up_buf, up_out, local_sems.at[11]))
        outputs[-1].start()

    def run_down_grad(unit, n, lanes):
        for part in range(2):
            columns = slice(part * width, (part + 1) * width)
            down_buf[:, columns] = dot(
                hid_kept[...], inputs[384:768, columns], ((0,), (0,))
            ).astype(BF16)
        outputs.append(pltpu.make_async_copy(down_buf, down_out, local_sems.at[12]))
        outputs[-1].start()

    steps = {
        "D": run_dispatch,
        "S": run_spread,
        "G": run_gather,
        "R": run_results,
        "Y": run_return,
        "M": run_mix,
        "WU": run_up_grad,
        "WD": run_down_grad,
    }
    for _, unit, _ in ORDER[:2]:
        prepare(unit)
    for kind, unit, n in ORDER:
        started[kind, unit, n] = steps[kind](unit, n, chunks[n])
    for index, copy in enumerate(copies):
        if index in relays:
            pl.when(relays[index])(copy.wait_send)
        else:
            copy.wait_send()
    for copy in outputs:
        copy.wait()
    assert len(copies) <= SEMS


def hand_over(*refs):
    count = 4
    sources, targets, held = refs[:4], refs[4:8], refs[8:12]
    sems = refs[12]
    arrive = [
        pltpu.make_async_copy(sources[item], held[item], sems.at[item]) for item in range(count)
    ]
    leave = [
        pltpu.make_async_copy(held[item], targets[item], sems.at[count + item])
        for item in range(count)
    ]
    for copy in arrive:
        copy.start()
    for item in range(count):
        arrive[item].wait()
        leave[item].start()
    for copy in leave:
        copy.wait()


def per_device(
    act_in,
    fresh_in,
    grad_in,
    fresh_grad,
    saved_input,
    expert_ids,
    slot_ids,
    gates,
    up_weight,
    down_weight,
):
    sections = lax.axis_size("pipe")
    tokens, features = fresh_in.shape
    width = features // QUARTERS
    hidden = up_weight.shape[2]
    place = (expert_ids * 8 + slot_ids).astype(F32)
    table = jnp.concatenate([place, gates], axis=1).reshape(8, tokens)
    regroup = regroup_matrix()
    anywhere = pl.BlockSpec(memory_space=pl.ANY)
    in_vmem = pl.BlockSpec(memory_space=pltpu.VMEM)
    full = (tokens, features)
    vm = pltpu.VMEM
    acts, grads, up_grad, down_grad = pl.pallas_call(
        functools.partial(kernel, sections, width, hidden),
        out_shape=(
            jax.ShapeDtypeStruct((2,) + full, BF16),
            jax.ShapeDtypeStruct((2,) + full, BF16),
            jax.ShapeDtypeStruct((2 * width, hidden), BF16),
            jax.ShapeDtypeStruct((hidden, 2 * width), BF16),
        ),
        in_specs=[anywhere] * 7 + [in_vmem] * 3,
        out_specs=[anywhere] * 4,
        scratch_shapes=[
            vm(full, BF16),
            vm(full, BF16),
            vm(full, BF16),
            vm(full, BF16),
            vm((2,) + full, BF16),
            vm((2 * width, hidden), BF16),
            vm((hidden, 2 * width), BF16),
            vm((4, 192, 128), BF16),
            vm((8, 128, width), BF16),
            vm((10, 144, width), BF16),
            vm((10, 192, width), BF16),
            vm((6, 4, 48, width), BF16),
            vm((6, 8, 48, width), BF16),
            vm((1152, 2 * width), BF16),
            vm((6, 192, hidden), F32),
            vm((6, 192, hidden), F32),
            vm((384, hidden), BF16),
            vm((384, hidden), BF16),
            vm((384, hidden), BF16),
            vm((4, 8, 48, width), BF16),
            vm((4, 8, 48, width), BF16),
            vm((4, 128, width), BF16),
            vm((2, 128, width), BF16),
            vm((2,) + full, BF16),
            vm((2,) + full, BF16),
            vm((2 * width, hidden), BF16),
            vm((hidden, 2 * width), BF16),
            pltpu.SemaphoreType.DMA((SEMS,)),
            pltpu.SemaphoreType.DMA((SEMS,)),
            pltpu.SemaphoreType.DMA((13,)),
        ],
        compiler_params=pltpu.CompilerParams(
            collective_id=0, has_side_effects=True, vmem_limit_bytes=60 * 2**20
        ),
    )(
        act_in[0],
        fresh_in,
        grad_in[0],
        fresh_grad,
        saved_input[:, 0],
        up_weight[0],
        down_weight[0],
        table,
        jnp.asarray(regroup, BF16),
        jnp.asarray(regroup.T, BF16),
    )
    results = (acts[:, None], grads[:, None], up_grad[None], down_grad[None])
    return pl.pallas_call(
        hand_over,
        out_shape=tuple(jax.ShapeDtypeStruct(item.shape, item.dtype) for item in results),
        in_specs=[anywhere] * 4,
        out_specs=[anywhere] * 4,
        scratch_shapes=[vm(item.shape, item.dtype) for item in results]
        + [pltpu.SemaphoreType.DMA((8,))],
        compiler_params=pltpu.CompilerParams(vmem_limit_bytes=60 * 2**20),
    )(*results)


def solution(mesh):
    in_specs = (
        P("pipe", ("expert", "dp"), None),
        P(("expert", "dp"), None),
        P("pipe", ("expert", "dp"), None),
        P(("expert", "dp"), None),
        P(None, "pipe", ("expert", "dp"), None),
        P("pipe", None, ("expert", "dp"), None),
        P("pipe", None, ("expert", "dp"), None),
        P("pipe", None, ("expert", "dp"), None),
        P("pipe", "dp", "expert"),
        P("pipe", "expert", "dp"),
    )
    out_specs = (
        P(None, "pipe", ("expert", "dp"), None),
        P(None, "pipe", ("expert", "dp"), None),
        P("pipe", "dp", "expert"),
        P("pipe", "expert", "dp"),
    )
    return jax.shard_map(
        per_device, mesh=mesh, in_specs=in_specs, out_specs=out_specs, check_vma=False
    )
```
